128 devices in a mesh: ax: 16 (over z, x), az: 8 (over y, core).
Axes of the slice: x: 4, y: 4, z: 4, core: 2. Of those that a mesh axis runs over, the one named last changes fastest.
Arguments:
- history: bfloat16 [8192, 3, 3, 16, 256], P(('ax', 'az')), may hold values from -6 to 6
- inverse_tiles: bfloat16 [8192, 128, 128], P(('ax', 'az')), may hold values from -0.22097087 to 1.2209709
- levels: int32 [8192], P(('ax', 'az')), may hold values from 0 to 2
- destination: int32 [8192], P(('ax', 'az')), may hold values from 0 to 8191, as said below
Outputs:
- new_field: float32 [8192, 3, 16, 256], P(('ax', 'az'))
The draws below stay inside these ranges and needn't reach their ends.
Inputs may be any that keep to these rules, and one draw needn't show every extreme that they name: `destination`: A permutation of all block places. The 64 blocks of one old owner go to exactly half of all devices as new owners, 1 block to each.
All inputs are finite; a program needn't handle non-finite values.
Results may differ from the reference program's by a relative error of at most 0.009.
Values may be sent and summed in bfloat16 or wider, within the bound.
A program may use at most 128 MiB of HBM per device.

```python
import jax
import jax.numpy as jnp

BE = 16
TW = 128
BPD = 64
NB = 8192
N_AX = 16
N_AZ = 8


def draw_tiles_body(key):
    key_off, key_diag = jax.random.split(jax.random.fold_in(key, 5))
    bound_off = 2.0 / TW ** 0.5
    off_part = jnp.clip(jax.random.normal(key_off, (NB, TW, TW), jnp.float32) * (0.5 / TW ** 0.5), -bound_off, bound_off)
    diagonal = jax.random.uniform(key_diag, (NB, TW), jnp.float32, 0.3, 1.0)
    return off_part + diagonal[:, :, None] * jnp.eye(TW, dtype=jnp.float32)[None]


def draw_inverse_tiles(key, part):
    return draw_tiles_body(key).astype(jnp.bfloat16)


def shuffle_one(local_key):
    return jax.random.permutation(local_key, BPD)


def draw_destination(key, part):
    device_count = NB // BPD
    groups = device_count // 2
    per_peer = BPD // groups
    key_order, key_offset, key_slot, key_local = jax.random.split(jax.random.fold_in(key, 17), 4)
    device_order = jax.random.permutation(key_order, device_count)
    device_rank = jnp.argsort(device_order)
    offsets = jax.random.permutation(key_offset, device_count)[:groups]
    owner_table = device_order[(device_rank[:, None] + offsets[None, :]) % device_count]
    slot_table = jax.random.permutation(key_slot, BPD).reshape(groups, per_peer)
    targets = (owner_table[:, :, None] * BPD + slot_table[None, :, :]).reshape(device_count, BPD)
    shuffles = jax.vmap(shuffle_one)(jax.random.split(key_local, device_count))
    targets = jnp.take_along_axis(targets, shuffles, axis=1)
    return targets.reshape(NB).astype(jnp.int32)


def plant(entries, own_key, least, largest):
    extent = entries.shape
    index_at = [jax.random.randint(jax.random.fold_in(own_key, axis), (), 0, extent[axis]) for axis in range(len(extent))]
    entries = entries.at[tuple(index_at)].set(least)
    longest = extent.index(max(extent))
    index_at[longest] = (index_at[longest] + 1) % extent[longest]
    return entries.at[tuple(index_at)].set(largest)


def steps_of(stream_key, dims, cuts, low, high):
    def one(dim, blocks):
        heights = jax.random.uniform(jax.random.fold_in(jax.random.fold_in(stream_key, 6), dim), (blocks,), jnp.float32, low / len(cuts), high / len(cuts))
        return jnp.repeat(jnp.exp(heights), dims[dim] // blocks).reshape((-1,) + (1,) * (len(dims) - dim - 1))

    loudness = one(*cuts[0])
    for cut in cuts[1:]:
        loudness = loudness * one(*cut)
    return loudness


def gaussian(key, dims, spread, reach, cuts=(), kind=jnp.bfloat16):
    values = jax.random.normal(key, dims, jnp.float32) * spread
    if len(cuts) > 0:
        values = steps_of(key, dims, cuts, -0.22, 0.18) * values
    return jnp.clip(values, min=-reach, max=reach).astype(kind)


def setup_inputs(seed: int = 0) -> dict:
    splits = jax.random.split(jax.random.key(seed), 5)
    history = gaussian(splits[0], (NB, 3, 3, BE, BE * BE), 1.0, 6.0, ((0, 128),))
    inverse_tiles = draw_inverse_tiles(jax.random.fold_in(splits[4], 71), 0)
    levels = plant(jax.random.randint(splits[2], (NB,), 0, 3), jax.random.fold_in(splits[2], 1), 0, 2).astype(jnp.int32)
    destination = draw_destination(jax.random.fold_in(splits[4], 71), 0)
    return {"history": history, "inverse_tiles": inverse_tiles, "levels": levels, "destination": destination}


diffusion = 0.04


def reference(history, inverse_tiles, levels, destination):
    arrived = jnp.zeros_like(history).at[destination].set(history)
    arrived_tiles = jnp.zeros_like(inverse_tiles).at[destination].set(inverse_tiles)
    level_scale = jnp.left_shift(jnp.ones_like(levels), 2 * levels).astype(jnp.float32)
    arrived_scale = jnp.zeros((NB,), jnp.float32).at[destination].set(level_scale)
    newest = arrived[:, 0].astype(jnp.float32)
    combined = 18.0 * newest - 9.0 * arrived[:, 1].astype(jnp.float32) + 2.0 * arrived[:, 2].astype(jnp.float32)
    source_term = (combined / 11.0).astype(jnp.bfloat16)
    grid = newest.reshape(N_AX, N_AZ, BPD, 3, BE, BE, BE).transpose(3, 4, 0, 5, 1, 2, 6)
    grid = grid.reshape(3, BE, N_AX * BE, N_AZ * BPD * BE)
    padded = jnp.pad(grid, ((0, 0), (1, 1), (1, 1), (0, 0)))
    beside_all = padded[:, 2:, 1:-1] + padded[:, :-2, 1:-1]
    beside_all = beside_all + padded[:, 1:-1, 2:] + padded[:, 1:-1, :-2]
    beside_all = beside_all + jnp.roll(grid, 1, axis=3) + jnp.roll(grid, -1, axis=3)
    neighbours = beside_all.reshape(3, BE, N_AX, BE, N_AZ, BPD, BE).transpose(2, 4, 5, 0, 1, 3, 6)
    neighbours = neighbours.reshape(NB, 3, BE, BE * BE)
    coupling = diffusion * arrived_scale[:, None, None, None]
    operated = (1.0 + 6.0 * coupling) * newest - coupling * neighbours
    defect = (source_term.astype(jnp.float32) - operated).astype(jnp.bfloat16)
    flat_defect = defect.astype(jnp.float32).reshape(NB, -1, TW)
    update = jnp.einsum("bpj,bij->bpi", flat_defect, arrived_tiles.astype(jnp.float32))
    return newest + update.reshape(newest.shape)
```

```python
import functools

import jax
import jax.numpy as jnp
from jax import lax
from jax.experimental import pallas as pl
from jax.experimental.pallas import tpu as pltpu
from jax.sharding import PartitionSpec as P

diffusion = 0.04
MESH = pl.DeviceIdType.MESH
F32 = jnp.float32
BF = jnp.bfloat16

BLOCKS = 64
DEVS = 128
AZ = 8
R1 = 80
STRIDE = 107
UNROLL = 4
NONE = 127


def target_of(ax, az, i):
    o = lax.rem(i * STRIDE, DEVS)
    dc = lax.rem(o, 2)
    dy = lax.rem(lax.div(o, 2), 4)
    dx = lax.rem(lax.div(o, 8), 4)
    dz = lax.div(o, 32)
    z = lax.rem(lax.div(ax, 4) + dz, 4)
    x = lax.rem(lax.rem(ax, 4) + dx, 4)
    y = lax.rem(lax.div(az, 2) + dy, 4)
    c = lax.rem(lax.rem(az, 2) + dc, 2)
    return z * 4 + x, y * 2 + c


def bf16_of(mask):
    return jnp.where(mask, 1.0, 0.0).astype(BF)


def fill_constants(nsel, tsel, weights, ax):
    src = lax.broadcasted_iota(jnp.int32, (256, 256), 0)
    dst = lax.broadcasted_iota(jnp.int32, (256, 256), 1)
    ps, qs = lax.div(src, 16), lax.rem(src, 16)
    pd, qd = lax.div(dst, 16), lax.rem(dst, 16)
    beside = ((ps == pd) & (jnp.abs(qs - qd) == 1)) | ((qs == qd) & (jnp.abs(ps - pd) == 1))
    nsel[:, 0:256] = bf16_of(beside)
    src = lax.broadcasted_iota(jnp.int32, (256, 128), 0)
    kk = lax.rem(lax.broadcasted_iota(jnp.int32, (256, 128), 1), 64)
    plane = jnp.where(kk < 48, 0, 8) + lax.rem(kk, 8)
    pick = jnp.where(
        kk < 16,
        240 + kk,
        jnp.where(kk < 32, kk - 16, plane * 16 + jnp.where(lax.rem(kk, 16) < 8, 15, 0)),
    )
    nsel[:, 256:384] = bf16_of(src == pick)
    row = lax.broadcasted_iota(jnp.int32, (48, 128), 0)
    col = lax.broadcasted_iota(jnp.int32, (48, 128), 1)
    pick = jnp.where(
        row < 16,
        row,
        jnp.where(row < 32, 96 + row, lax.rem(row, 8) * 16 + jnp.where(row < 40, 0, 15)),
    )
    tsel[...] = bf16_of(col == pick)
    kk = lax.rem(lax.broadcasted_iota(jnp.int32, (16, 128), 1), 64)
    weights[0] = bf16_of((kk < 16) & (ax > 0))
    weights[1] = bf16_of((kk >= 16) & (kk < 32) & (ax < 15))
    weights[2] = bf16_of((kk >= 32) & (lax.rem(kk, 16) < 8))
    weights[3] = bf16_of((kk >= 32) & (lax.rem(kk, 16) >= 8))


def kernel(
    hist, tiles, dest, lev, out,
    hbuf, tbuf, msg1, send1, recv1, base, send_a, recv_a, send_b, recv_b, stage, ordf,
    nsel, tsel, weights, vidx, sidx, vinv, sinv, meta_s, meta_r,
    load_sem, ssem, rsem, out_sem,
):
    ax = lax.axis_index("ax")
    az = lax.axis_index("az")
    me = ax * AZ + az
    barrier = pltpu.get_barrier_semaphore()

    def greet(i, carry):
        pl.semaphore_signal(barrier, inc=1, device_id=target_of(ax, az, i), device_id_type=MESH)
        return carry

    lax.fori_loop(1, DEVS, greet, 0)

    load_h = pltpu.make_async_copy(hist, hbuf, load_sem.at[0])
    load_t = pltpu.make_async_copy(tiles, tbuf, load_sem.at[1])
    load_h.start()
    load_t.start()

    lane = lax.broadcasted_iota(jnp.int32, (1, 128), 1)

    def place(b, carry):
        which, slot = carry
        there = dest[b]
        hit = lane == lax.div(there, BLOCKS)
        return jnp.where(hit, b, which), jnp.where(hit, lax.rem(there, BLOCKS), slot)

    which, slot = lax.fori_loop(
        0, BLOCKS, place, (jnp.zeros((1, 128), jnp.int32), jnp.full((1, 128), NONE, jnp.int32))
    )
    vidx[0:1, :] = which
    vidx[1:2, :] = slot
    to_smem = pltpu.make_async_copy(vidx, sidx, load_sem.at[2])
    to_smem.start()
    fill_constants(nsel, tsel, weights, ax)
    to_smem.wait()

    lanes16 = lax.broadcasted_iota(jnp.int32, (16, 128), 1)

    def one_block(b):
        x = hbuf[b, 0:3].reshape(48, 256)
        y = jnp.dot(x, nsel[...], preferred_element_type=F32)
        h0 = x.astype(F32)
        h1 = hbuf[b, 3:6].reshape(48, 256).astype(F32)
        h2 = hbuf[b, 6:9].reshape(48, 256).astype(F32)
        source = ((18.0 * h0 - 9.0 * h1 + 2.0 * h2) * (1.0 / 11.0)).astype(BF).astype(F32)
        level = lev[b]
        scale = jnp.where(level == 0, 1.0, jnp.where(level == 1, 4.0, 16.0)).astype(F32)
        c = diffusion * scale
        radial = lax.rem(lax.broadcasted_iota(jnp.int32, (48, 256), 0), 16)
        beside = y[:, 0:256]
        beside += jnp.where(radial == 0, 0.0, pltpu.roll(h0, 1, 0))
        beside += jnp.where(radial == 15, 0.0, pltpu.roll(h0, 47, 0))
        defect = (source - (1.0 + 6.0 * c) * h0 + c * beside).astype(BF)
        lhs = jnp.concatenate([defect[:, 0:128], defect[:, 128:256], tsel[...]], axis=0)
        u = lax.dot_general(lhs, tbuf[b], (((1,), (1,)), ((), ())), preferred_element_type=F32)
        moved = h0 + jnp.concatenate([u[0:48], u[48:96]], axis=1)
        base[b] = moved.astype(BF).reshape(3, 16, 256)
        msg1[b, 0:48] = (u[96:144] * scale).astype(BF)
        faces = y[:, 256:384]
        msg1[b, 48:64] = jnp.where(lanes16 < 64, faces[0:16], faces[16:32]).astype(BF)
        msg1[b, 64:80] = faces[32:48].astype(BF)

    load_h.wait()
    load_t.wait()

    def some_blocks(n, carry):
        for k in range(UNROLL):
            one_block(n * UNROLL + k)
        return carry

    lax.fori_loop(0, BLOCKS // UNROLL, some_blocks, 0)

    kk16 = lax.rem(lanes16, 64)

    def pack_first(d, meta, first):
        below = jnp.where(d >= AZ, d - AZ, d)
        above = jnp.where(d < DEVS - AZ, d + AZ, d)
        slot_below = jnp.where(d >= AZ, sidx[1, below], NONE)
        slot_above = jnp.where(d < DEVS - AZ, sidx[1, above], NONE)
        meta[d] = jnp.where(lane < 64, sidx[1, d], slot_below * 128 + slot_above)
        own, low, high = sidx[0, d], sidx[0, below], sidx[0, above]
        first[d, 0:48] = msg1[own, 0:48]
        for r in (48, 64):
            first[d, r : r + 16] = jnp.where(
                kk16 < 16,
                msg1[low, r : r + 16].astype(F32),
                jnp.where(
                    kk16 < 32, msg1[high, r : r + 16].astype(F32), msg1[own, r : r + 16].astype(F32)
                ),
            ).astype(BF)

    pack_first(me, meta_r, recv1)
    own = sidx[0, me]
    recv_a[me] = base[own, 0:2]
    recv_b[me] = base[own, 2:3]

    pl.semaphore_wait(barrier, DEVS - 1)

    def push(src, dst, n, where):
        pltpu.make_async_remote_copy(
            src_ref=src, dst_ref=dst, send_sem=ssem.at[n], recv_sem=rsem.at[n],
            device_id=where, device_id_type=MESH,
        ).start()

    def send_first(i, carry):
        tax, taz = target_of(ax, az, i)
        d = tax * AZ + taz
        pack_first(d, meta_s, send1)
        push(meta_s.at[d], meta_r.at[me], 0, (tax, taz))
        push(send1.at[d], recv1.at[me], 1, (tax, taz))
        return carry

    lax.fori_loop(1, DEVS, send_first, 0)

    def send_base(n, send, recv, low, high):
        def one(i, carry):
            tax, taz = target_of(ax, az, i)
            d = tax * AZ + taz
            send[d] = base[sidx[0, d], low:high]
            push(send.at[d], recv.at[me], n, (tax, taz))
            return carry

        lax.fori_loop(1, DEVS, one, 0)

    send_base(2, send_a, recv_a, 0, 2)

    def all_of(ref, sem):
        part = ref.at[pl.ds(0, DEVS - 1)]
        pltpu.make_async_copy(part, part, sem).wait()

    all_of(meta_r, rsem.at[0])

    def unplace(s, carry):
        mine, low, high = carry
        code = meta_r[s]
        mine = jnp.where(code == lane, s, mine)
        low = jnp.where(lax.div(code, 128) == lane - 64, s, low)
        high = jnp.where(lax.rem(code, 128) == lane - 64, s, high)
        return mine, low, high

    zero = jnp.zeros((1, 128), jnp.int32)
    mine, low, high = lax.fori_loop(0, DEVS, unplace, (zero, zero, zero))
    vinv[0:1, :] = mine
    vinv[1:2, :] = low
    vinv[2:3, :] = high
    to_smem = pltpu.make_async_copy(vinv, sinv, load_sem.at[2])
    to_smem.start()
    to_smem.wait()

    all_of(recv1, rsem.at[1])

    def order(j, carry):
        ordf[j + 1] = recv1[sinv[0, j], 48:80]
        return carry

    lax.fori_loop(0, BLOCKS, order, 0)
    edge_up = pltpu.make_async_remote_copy(
        src_ref=ordf.at[BLOCKS], dst_ref=ordf.at[0], send_sem=ssem.at[4], recv_sem=rsem.at[4],
        device_id=(ax, lax.rem(az + 1, AZ)), device_id_type=MESH,
    )
    edge_down = pltpu.make_async_remote_copy(
        src_ref=ordf.at[1], dst_ref=ordf.at[BLOCKS + 1], send_sem=ssem.at[5], recv_sem=rsem.at[5],
        device_id=(ax, lax.rem(az + AZ - 1, AZ)), device_id_type=MESH,
    )
    edge_up.start()
    edge_down.start()

    send_base(3, send_b, recv_b, 2, 3)
    edge_up.wait_recv()
    edge_down.wait_recv()

    def correct(j):
        s, s_low, s_high = sinv[0, j], sinv[1, j + 64], sinv[2, j + 64]
        parts = []
        for r in (0, 16):
            parts.append(
                recv1[s_low, 48 + r : 64 + r] * weights[0]
                + recv1[s_high, 48 + r : 64 + r] * weights[1]
                + ordf[j, r : r + 16] * weights[2]
                + ordf[j + 2, r : r + 16] * weights[3]
            )
        lhs = jnp.concatenate([parts[0][:, 0:64], parts[0][:, 64:128], parts[1][:, 0:64]], axis=0)
        none = jnp.zeros((16, 128), BF)
        t_low, t_high, t_side = recv1[s, 0:16], recv1[s, 16:32], recv1[s, 32:48]
        rhs = jnp.concatenate(
            [
                jnp.concatenate([t_low, none, t_side, none], axis=0),
                jnp.concatenate([none, t_high, none, t_side], axis=0),
            ],
            axis=1,
        )
        update = jnp.dot(lhs, rhs, preferred_element_type=F32) * diffusion
        stage[j] = update.reshape(3, 16, 256)

    def some_corrections(n, carry):
        for k in range(UNROLL):
            correct(n * UNROLL + k)
        return carry

    lax.fori_loop(0, BLOCKS // UNROLL, some_corrections, 0)

    all_of(recv_a, rsem.at[2])

    def add_a(n, carry):
        for k in range(UNROLL):
            j = n * UNROLL + k
            stage[j, 0:2] += recv_a[sinv[0, j]].astype(F32)
        return carry

    lax.fori_loop(0, BLOCKS // UNROLL, add_a, 0)
    all_of(recv_b, rsem.at[3])

    def add_b(n, carry):
        for k in range(UNROLL):
            j = n * UNROLL + k
            stage[j, 2:3] += recv_b[sinv[0, j]].astype(F32)
        return carry

    copies = []
    for g in range(4):
        lax.fori_loop(g * 16 // UNROLL, (g + 1) * 16 // UNROLL, add_b, 0)
        part = pl.ds(g * 16, 16)
        copies.append(pltpu.make_async_copy(stage.at[part], out.at[part], out_sem.at[g]))
        copies[-1].start()

    all_of(meta_s, ssem.at[0])
    all_of(send1, ssem.at[1])
    all_of(send_a, ssem.at[2])
    all_of(send_b, ssem.at[3])
    edge_up.wait_send()
    edge_down.wait_send()
    for copy in copies:
        copy.wait()


def body(history, inverse_tiles, levels, destination):
    anywhere = pl.BlockSpec(memory_space=pl.ANY)
    scalars = pl.BlockSpec(memory_space=pltpu.SMEM)
    return pl.pallas_call(
        kernel,
        out_shape=jax.ShapeDtypeStruct((BLOCKS, 3, 16, 256), F32),
        in_specs=[anywhere, anywhere, scalars, scalars],
        out_specs=anywhere,
        scratch_shapes=[
            pltpu.VMEM((BLOCKS, 9, 16, 256), BF),
            pltpu.VMEM((BLOCKS, 128, 128), BF),
            pltpu.VMEM((BLOCKS, R1, 128), BF),
            pltpu.VMEM((DEVS, R1, 128), BF),
            pltpu.VMEM((DEVS, R1, 128), BF),
            pltpu.VMEM((BLOCKS, 3, 16, 256), BF),
            pltpu.VMEM((DEVS, 2, 16, 256), BF),
            pltpu.VMEM((DEVS, 2, 16, 256), BF),
            pltpu.VMEM((DEVS, 1, 16, 256), BF),
            pltpu.VMEM((DEVS, 1, 16, 256), BF),
            pltpu.VMEM((BLOCKS, 3, 16, 256), F32),
            pltpu.VMEM((BLOCKS + 2, 32, 128), BF),
            pltpu.VMEM((256, 384), BF),
            pltpu.VMEM((48, 128), BF),
            pltpu.VMEM((4, 16, 128), BF),
            pltpu.VMEM((8, 128), jnp.int32),
            pltpu.SMEM((8, 128), jnp.int32),
            pltpu.VMEM((8, 128), jnp.int32),
            pltpu.SMEM((8, 128), jnp.int32),
            pltpu.VMEM((DEVS, 1, 128), jnp.int32),
            pltpu.VMEM((DEVS, 1, 128), jnp.int32),
            pltpu.SemaphoreType.DMA((3,)),
            pltpu.SemaphoreType.DMA((6,)),
            pltpu.SemaphoreType.DMA((6,)),
            pltpu.SemaphoreType.DMA((4,)),
        ],
        compiler_params=pltpu.CompilerParams(
            collective_id=0, has_side_effects=True, vmem_limit_bytes=48 * 2**20
        ),
    )(history.reshape(BLOCKS, 9, 16, 256), inverse_tiles, destination, levels)


def solution(mesh):
    placed = (
        P(("ax", "az"), None, None, None, None),
        P(("ax", "az"), None, None),
        P(("ax", "az")),
        P(("ax", "az")),
    )
    return jax.shard_map(
        body,
        mesh=mesh,
        in_specs=placed,
        out_specs=P(("ax", "az"), None, None, None),
        check_vma=False,
    )
```

```python
import functools

import jax
import jax.numpy as jnp
from jax import lax
from jax.experimental import pallas as pl
from jax.experimental.pallas import tpu as pltpu
from jax.sharding import PartitionSpec as P

diffusion = 0.04
MESH = pl.DeviceIdType.MESH
F32 = jnp.float32
BF = jnp.bfloat16

BLOCKS = 64
DEVS = 128
AZ = 8
R1 = 80
STRIDE = 107
UNROLL = 4
NONE = 127


def target_of(ax, az, i):
    o = lax.rem(i * STRIDE, DEVS)
    dc = lax.rem(o, 2)
    dy = lax.rem(lax.div(o, 2), 4)
    dx = lax.rem(lax.div(o, 8), 4)
    dz = lax.div(o, 32)
    z = lax.rem(lax.div(ax, 4) + dz, 4)
    x = lax.rem(lax.rem(ax, 4) + dx, 4)
    y = lax.rem(lax.div(az, 2) + dy, 4)
    c = lax.rem(lax.rem(az, 2) + dc, 2)
    return z * 4 + x, y * 2 + c


def bf16_of(mask):
    return jnp.where(mask, 1.0, 0.0).astype(BF)


def fill_constants(nsel, fsel, tsel, weights, ax):
    src = lax.broadcasted_iota(jnp.int32, (256, 256), 0)
    dst = lax.broadcasted_iota(jnp.int32, (256, 256), 1)
    ps, qs = lax.div(src, 16), lax.rem(src, 16)
    pd, qd = lax.div(dst, 16), lax.rem(dst, 16)
    beside = ((ps == pd) & (jnp.abs(qs - qd) == 1)) | ((qs == qd) & (jnp.abs(ps - pd) == 1))
    nsel[...] = bf16_of(beside)
    src = lax.broadcasted_iota(jnp.int32, (256, 128), 0)
    kk = lax.rem(lax.broadcasted_iota(jnp.int32, (256, 128), 1), 64)
    plane = jnp.where(kk < 48, 0, 8) + lax.rem(kk, 8)
    pick = jnp.where(
        kk < 16,
        240 + kk,
        jnp.where(kk < 32, kk - 16, plane * 16 + jnp.where(lax.rem(kk, 16) < 8, 15, 0)),
    )
    low, high = kk < 16, (kk >= 16) & (kk < 32)
    fsel[0] = bf16_of((src == pick) & low)
    fsel[1] = bf16_of((src == pick) & high)
    fsel[2] = bf16_of((src == pick) & (kk >= 32))
    row = lax.broadcasted_iota(jnp.int32, (48, 128), 0)
    col = lax.broadcasted_iota(jnp.int32, (48, 128), 1)
    pick = jnp.where(
        row < 16,
        row,
        jnp.where(row < 32, 96 + row, lax.rem(row, 8) * 16 + jnp.where(row < 40, 0, 15)),
    )
    tsel[...] = bf16_of(col == pick)
    kk = lax.rem(lax.broadcasted_iota(jnp.int32, (16, 128), 1), 64)
    weights[0] = bf16_of((kk < 16) & (ax > 0))
    weights[1] = bf16_of((kk >= 16) & (kk < 32) & (ax < 15))
    weights[2] = bf16_of((kk >= 32) & (lax.rem(kk, 16) < 8))
    weights[3] = bf16_of((kk >= 32) & (lax.rem(kk, 16) >= 8))


def kernel(
    hist, tiles, dest_any, lev_any, out,
    newest, older, tbuf, send1, recv1, base, send_a, recv_a, send_b, recv_b, stage, final, ordf,
    nsel, fsel, tsel, weights, dest, lev, vidx, sidx, vinv, sinv,
    load_sem, ssem, rsem, out_sem,
):
    ax = lax.axis_index("ax")
    az = lax.axis_index("az")
    me = ax * AZ + az
    barrier = pltpu.get_barrier_semaphore()

    load_d = pltpu.make_async_copy(dest_any, dest, load_sem.at[3])
    load_l = pltpu.make_async_copy(lev_any, lev, load_sem.at[4])
    load_h0 = pltpu.make_async_copy(hist.at[:, pl.ds(0, 3)], newest, load_sem.at[0])
    load_h = pltpu.make_async_copy(hist.at[:, pl.ds(3, 6)], older, load_sem.at[5])
    load_t = pltpu.make_async_copy(tiles, tbuf, load_sem.at[1])
    loads = (load_d, load_l, load_h0, load_t, load_h)
    for load in loads:
        load.start()

    def greet(i, carry):
        t = lax.rem(me + i, DEVS)
        there = (lax.div(t, AZ), lax.rem(t, AZ))
        pl.semaphore_signal(barrier, inc=1, device_id=there, device_id_type=MESH)
        return carry

    lax.fori_loop(1, DEVS, greet, 0)

    lane = lax.broadcasted_iota(jnp.int32, (1, 128), 1)

    def place(b, carry):
        which, slot = carry
        there = dest[b]
        hit = lane == lax.div(there, BLOCKS)
        return jnp.where(hit, b, which), jnp.where(hit, lax.rem(there, BLOCKS), slot)

    load_d.wait()
    load_l.wait()
    which, slot = lax.fori_loop(
        0, BLOCKS, place, (jnp.zeros((1, 128), jnp.int32), jnp.full((1, 128), NONE, jnp.int32))
    )
    vidx[0:1, :] = which
    vidx[1:2, :] = slot
    to_smem = pltpu.make_async_copy(vidx, sidx, load_sem.at[2])
    to_smem.start()
    fill_constants(nsel, fsel, tsel, weights, ax)
    to_smem.wait()

    lanes16 = lax.broadcasted_iota(jnp.int32, (16, 128), 1)

    def scale_of(b):
        level = lev[b]
        return jnp.where(level == 0, 1.0, jnp.where(level == 1, 4.0, 16.0)).astype(F32)

    def base_part(b):
        x = newest[b].reshape(48, 256)
        h0 = x.astype(F32)
        h1 = older[b, 0:3].reshape(48, 256).astype(F32)
        h2 = older[b, 3:6].reshape(48, 256).astype(F32)
        source = ((18.0 * h0 - 9.0 * h1 + 2.0 * h2) * (1.0 / 11.0)).astype(BF).astype(F32)
        c = diffusion * scale_of(b)
        radial = lax.rem(lax.broadcasted_iota(jnp.int32, (48, 256), 0), 16)
        beside = jnp.dot(x, nsel[...], preferred_element_type=F32)
        beside += jnp.where(radial == 0, 0.0, pltpu.roll(h0, 1, 0))
        beside += jnp.where(radial == 15, 0.0, pltpu.roll(h0, 47, 0))
        defect = (source - (1.0 + 6.0 * c) * h0 + c * beside).astype(BF)
        lhs = jnp.concatenate([defect[:, 0:128], defect[:, 128:256]], axis=0)
        u = lax.dot_general(lhs, tbuf[b], (((1,), (1,)), ((), ())), preferred_element_type=F32)
        moved = h0 + jnp.concatenate([u[0:48], u[48:96]], axis=1)
        base[b] = moved.astype(BF).reshape(3, 16, 256)

    def for_each(count, step):
        def some(n, carry):
            for k in range(UNROLL):
                step(n * UNROLL + k)
            return carry

        lax.fori_loop(0, count // UNROLL, some, 0)

    row16 = lax.broadcasted_iota(jnp.int32, (16, 128), 0)

    def pack_first(d):
        below = jnp.maximum(d - AZ, 0)
        above = jnp.minimum(d + AZ, DEVS - 1)
        slot_below = jnp.where(d >= AZ, sidx[1, below], NONE)
        slot_above = jnp.where(d < DEVS - AZ, sidx[1, above], NONE)
        slots = jnp.where(row16 == 0, sidx[1, d], jnp.where(row16 == 1, slot_below, slot_above))
        own, low, high = sidx[0, d], sidx[0, below], sidx[0, above]
        u = lax.dot_general(tsel[...], tbuf[own], (((1,), (1,)), ((), ())), preferred_element_type=F32)
        send1[d, 0:48] = (u * scale_of(own)).astype(BF)
        faces = sum(
            jnp.dot(newest[b].reshape(48, 256), fsel[n], preferred_element_type=F32)
            for n, b in enumerate((low, high, own))
        )
        send1[d, 48:64] = jnp.where(lanes16 < 64, faces[0:16], faces[16:32]).astype(BF)
        send1[d, 64:80] = jnp.where(lanes16 < 64, faces[32:48], slots.astype(F32)).astype(BF)

    def push(src, dst, n, where):
        pltpu.make_async_remote_copy(
            src_ref=src, dst_ref=dst, send_sem=ssem.at[n], recv_sem=rsem.at[n],
            device_id=where, device_id_type=MESH,
        ).start()

    load_h0.wait()
    load_t.wait()
    pl.semaphore_wait(barrier, DEVS - 1)

    def send_first(n, carry):
        targets = [target_of(ax, az, n * UNROLL + k) for k in range(UNROLL)]
        for tax, taz in targets:
            pack_first(tax * AZ + taz)
        for k, (tax, taz) in enumerate(targets):
            if k > 0:
                push(send1.at[tax * AZ + taz], recv1.at[me], 1, (tax, taz))
            else:

                @pl.when(n > 0)
                def _():
                    push(send1.at[tax * AZ + taz], recv1.at[me], 1, (tax, taz))

        return carry

    lax.fori_loop(0, DEVS // UNROLL, send_first, 0)
    recv1[me] = send1[me]

    load_h.wait()
    for_each(BLOCKS, base_part)
    own = sidx[0, me]
    recv_a[me] = base[own, 0:2]
    recv_b[me] = base[own, 2:3]

    def send_base(n, send, recv, low, high):
        def one(i, carry):
            tax, taz = target_of(ax, az, i)
            d = tax * AZ + taz
            send[d] = base[sidx[0, d], low:high]
            push(send.at[d], recv.at[me], n, (tax, taz))
            return carry

        lax.fori_loop(1, DEVS, one, 0)

    send_base(2, send_a, recv_a, 0, 2)

    def all_of(ref, sem):
        part = ref.at[pl.ds(0, DEVS - 1)]
        pltpu.make_async_copy(part, part, sem).wait()

    all_of(recv1, rsem.at[1])

    slot_of_lane = (lanes16 - 64).astype(F32)

    def unplace(n, found):
        for k in range(UNROLL):
            s = n * UNROLL + k
            found = jnp.where(recv1[s, 64:80].astype(F32) == slot_of_lane, s, found)
        return found

    vinv[...] = lax.fori_loop(0, DEVS // UNROLL, unplace, jnp.zeros((16, 128), jnp.int32))
    to_smem = pltpu.make_async_copy(vinv, sinv, load_sem.at[2])
    to_smem.start()
    to_smem.wait()

    def order(j):
        ordf[j + 1] = recv1[sinv[0, j + 64], 48:80]

    for_each(BLOCKS, order)
    edge_up = pltpu.make_async_remote_copy(
        src_ref=ordf.at[BLOCKS], dst_ref=ordf.at[0], send_sem=ssem.at[4], recv_sem=rsem.at[4],
        device_id=(ax, lax.rem(az + 1, AZ)), device_id_type=MESH,
    )
    edge_down = pltpu.make_async_remote_copy(
        src_ref=ordf.at[1], dst_ref=ordf.at[BLOCKS + 1], send_sem=ssem.at[5], recv_sem=rsem.at[5],
        device_id=(ax, lax.rem(az + AZ - 1, AZ)), device_id_type=MESH,
    )
    edge_up.start()
    edge_down.start()

    send_base(3, send_b, recv_b, 2, 3)
    edge_up.wait_recv()
    edge_down.wait_recv()

    def correct(j):
        s, s_low, s_high = sinv[0, j + 64], sinv[1, j + 64], sinv[2, j + 64]
        parts = []
        for r in (0, 16):
            parts.append(
                recv1[s_low, 48 + r : 64 + r] * weights[0]
                + recv1[s_high, 48 + r : 64 + r] * weights[1]
                + ordf[j, r : r + 16] * weights[2]
                + ordf[j + 2, r : r + 16] * weights[3]
            )
        lhs = jnp.concatenate([parts[0][:, 0:64], parts[0][:, 64:128], parts[1][:, 0:64]], axis=0)
        none = jnp.zeros((16, 128), BF)
        t_low, t_high, t_side = recv1[s, 0:16], recv1[s, 16:32], recv1[s, 32:48]
        rhs = jnp.concatenate(
            [
                jnp.concatenate([t_low, none, t_side, none], axis=0),
                jnp.concatenate([none, t_high, none, t_side], axis=0),
            ],
            axis=1,
        )
        update = jnp.dot(lhs, rhs, preferred_element_type=F32) * diffusion
        stage[j] = update.reshape(3, 16, 256)

    for_each(BLOCKS, correct)

    all_of(recv_a, rsem.at[2])

    def add_a(j):
        final[j, 0:2] = (stage[j, 0:2] + recv_a[sinv[0, j + 64]].astype(F32)).astype(BF)

    for_each(BLOCKS, add_a)
    all_of(recv_b, rsem.at[3])

    def add_b(n, carry):
        for k in range(UNROLL):
            j = n * UNROLL + k
            final[j, 2:3] = (stage[j, 2:3] + recv_b[sinv[0, j + 64]].astype(F32)).astype(BF)
        return carry

    copies = []
    for g in range(4):
        lax.fori_loop(g * 16 // UNROLL, (g + 1) * 16 // UNROLL, add_b, 0)
        part = pl.ds(g * 16, 16)
        copies.append(pltpu.make_async_copy(final.at[part], out.at[part], out_sem.at[g]))
        copies[-1].start()

    all_of(send1, ssem.at[1])
    all_of(send_a, ssem.at[2])
    all_of(send_b, ssem.at[3])
    edge_up.wait_send()
    edge_down.wait_send()
    for copy in copies:
        copy.wait()


def body(history, inverse_tiles, levels, destination):
    anywhere = pl.BlockSpec(memory_space=pl.ANY)
    moved = pl.pallas_call(
        kernel,
        out_shape=jax.ShapeDtypeStruct((BLOCKS, 3, 16, 256), BF),
        in_specs=[pl.BlockSpec(memory_space=pltpu.HBM)] * 4,
        out_specs=anywhere,
        scratch_shapes=[
            pltpu.VMEM((BLOCKS, 3, 16, 256), BF),
            pltpu.VMEM((BLOCKS, 6, 16, 256), BF),
            pltpu.VMEM((BLOCKS, 128, 128), BF),
            pltpu.VMEM((DEVS, R1, 128), BF),
            pltpu.VMEM((DEVS, R1, 128), BF),
            pltpu.VMEM((BLOCKS, 3, 16, 256), BF),
            pltpu.VMEM((DEVS, 2, 16, 256), BF),
            pltpu.VMEM((DEVS, 2, 16, 256), BF),
            pltpu.VMEM((DEVS, 1, 16, 256), BF),
            pltpu.VMEM((DEVS, 1, 16, 256), BF),
            pltpu.VMEM((BLOCKS, 3, 16, 256), F32),
            pltpu.VMEM((BLOCKS, 3, 16, 256), BF),
            pltpu.VMEM((BLOCKS + 2, 32, 128), BF),
            pltpu.VMEM((256, 256), BF),
            pltpu.VMEM((3, 256, 128), BF),
            pltpu.VMEM((48, 128), BF),
            pltpu.VMEM((4, 16, 128), BF),
            pltpu.SMEM((BLOCKS,), jnp.int32),
            pltpu.SMEM((BLOCKS,), jnp.int32),
            pltpu.VMEM((8, 128), jnp.int32),
            pltpu.SMEM((8, 128), jnp.int32),
            pltpu.VMEM((16, 128), jnp.int32),
            pltpu.SMEM((16, 128), jnp.int32),
            pltpu.SemaphoreType.DMA((6,)),
            pltpu.SemaphoreType.DMA((6,)),
            pltpu.SemaphoreType.DMA((6,)),
            pltpu.SemaphoreType.DMA((4,)),
        ],
        compiler_params=pltpu.CompilerParams(
            collective_id=0, has_side_effects=True, vmem_limit_bytes=60 * 2**20
        ),
    )(history.reshape(BLOCKS, 9, 16, 256), inverse_tiles, destination, levels)
    return moved.astype(F32)


def solution(mesh):
    placed = (
        P(("ax", "az"), None, None, None, None),
        P(("ax", "az"), None, None),
        P(("ax", "az")),
        P(("ax", "az")),
    )
    return jax.shard_map(
        body,
        mesh=mesh,
        in_specs=placed,
        out_specs=P(("ax", "az"), None, None, None),
        check_vma=False,
    )
```

```python
import functools

import jax
import jax.numpy as jnp
from jax import lax
from jax.experimental import pallas as pl
from jax.experimental.pallas import tpu as pltpu
from jax.sharding import PartitionSpec as P

diffusion = 0.04
MESH = pl.DeviceIdType.MESH
F32 = jnp.float32
BF = jnp.bfloat16

BLOCKS = 64
DEVS = 128
AZ = 8
FACES = 24
EARLY = 44
STRIDE = 107
UNROLL = 4
CUTS = (4, 16)
GROUPS = 3
GROUP = (DEVS - EARLY) // GROUPS
NONE = 127


def target_of(ax, az, i):
    o = lax.rem(i * STRIDE, DEVS)
    dc = lax.rem(o, 2)
    dy = lax.rem(lax.div(o, 2), 4)
    dx = lax.rem(lax.div(o, 8), 4)
    dz = lax.div(o, 32)
    z = lax.rem(lax.div(ax, 4) + dz, 4)
    x = lax.rem(lax.rem(ax, 4) + dx, 4)
    y = lax.rem(lax.div(az, 2) + dy, 4)
    c = lax.rem(lax.rem(az, 2) + dc, 2)
    return z * 4 + x, y * 2 + c


def source_of(ax, az, i):
    o = lax.rem(i * STRIDE, DEVS)
    dc = lax.rem(o, 2)
    dy = lax.rem(lax.div(o, 2), 4)
    dx = lax.rem(lax.div(o, 8), 4)
    dz = lax.div(o, 32)
    z = lax.rem(lax.div(ax, 4) - dz + 4, 4)
    x = lax.rem(lax.rem(ax, 4) - dx + 4, 4)
    y = lax.rem(lax.div(az, 2) - dy + 4, 4)
    c = lax.rem(lax.rem(az, 2) - dc + 2, 2)
    return z * 4 + x, y * 2 + c


def bf16_of(mask):
    return jnp.where(mask, 1.0, 0.0).astype(BF)


def fill_constants(nsel, fsel, spread, tsel, weights, ax):
    src = lax.broadcasted_iota(jnp.int32, (256, 256), 0)
    dst = lax.broadcasted_iota(jnp.int32, (256, 256), 1)
    ps, qs = lax.div(src, 16), lax.rem(src, 16)
    pd, qd = lax.div(dst, 16), lax.rem(dst, 16)
    beside = ((ps == pd) & (jnp.abs(qs - qd) == 1)) | ((qs == qd) & (jnp.abs(ps - pd) == 1))
    nsel[...] = bf16_of(beside)
    src = lax.broadcasted_iota(jnp.int32, (256, 128), 0)
    kk = lax.rem(lax.broadcasted_iota(jnp.int32, (256, 128), 1), 64)
    plane = jnp.where(kk < 48, 0, 8) + lax.rem(kk, 8)
    pick = jnp.where(
        kk < 16,
        240 + kk,
        jnp.where(kk < 32, kk - 16, plane * 16 + jnp.where(lax.rem(kk, 16) < 8, 15, 0)),
    )
    low, high = kk < 16, (kk >= 16) & (kk < 32)
    fsel[0] = bf16_of((src == pick) & low)
    fsel[1] = bf16_of((src == pick) & high)
    fsel[2] = bf16_of((src == pick) & (kk >= 32))
    row = lax.broadcasted_iota(jnp.int32, (48, 128), 0)
    col = lax.broadcasted_iota(jnp.int32, (48, 128), 1)
    pick = jnp.where(
        row < 16,
        row,
        jnp.where(row < 32, 96 + row, lax.rem(row, 8) * 16 + jnp.where(row < 40, 0, 15)),
    )
    tsel[...] = bf16_of(col == pick)
    kk = lax.broadcasted_iota(jnp.int32, (64, 256), 0)
    dst = lax.broadcasted_iota(jnp.int32, (64, 256), 1)
    plane = jnp.where(kk < 48, 0, 8) + lax.rem(kk, 8)
    pick = jnp.where(
        kk < 16,
        kk,
        jnp.where(kk < 32, 224 + kk, plane * 16 + jnp.where(lax.rem(kk, 16) < 8, 0, 15)),
    )
    spread[...] = bf16_of(dst == pick)
    kk = lax.rem(lax.broadcasted_iota(jnp.int32, (FACES, 128), 1), 64)
    weights[0] = bf16_of((kk < 16) & (ax > 0))
    weights[1] = bf16_of((kk >= 16) & (kk < 32) & (ax < 15))
    weights[2] = bf16_of((kk >= 32) & (lax.rem(kk, 16) < 8))
    weights[3] = bf16_of((kk >= 32) & (lax.rem(kk, 16) >= 8))


def kernel(
    hist, tiles, dest_any, lev_any, out,
    newest, older, tbuf, meta_s, meta_r, send1, recv1, send_t, recv_t, send2, recv2, base,
    send_a, recv_a, send_b, recv_b, stage, final, ordf, beside_faces,
    nsel, fsel, spread, tsel, weights, dest, lev, vidx, sidx, vinv, sinv,
    load_sem, ssem, rsem, back_sem, out_sem,
):
    ax = lax.axis_index("ax")
    az = lax.axis_index("az")
    me = ax * AZ + az
    barrier = pltpu.get_barrier_semaphore()

    load_d = pltpu.make_async_copy(dest_any, dest, load_sem.at[3])
    load_l = pltpu.make_async_copy(lev_any, lev, load_sem.at[4])
    load_h0 = pltpu.make_async_copy(hist.at[:, pl.ds(0, 3)], newest, load_sem.at[0])
    load_h = pltpu.make_async_copy(hist.at[:, pl.ds(3, 6)], older, load_sem.at[5])
    load_t = pltpu.make_async_copy(tiles, tbuf, load_sem.at[1])
    loads = (load_d, load_l, load_h0, load_t, load_h)
    for load in loads:
        load.start()

    def greet(i, carry):
        t = lax.rem(me + i, DEVS)
        there = (lax.div(t, AZ), lax.rem(t, AZ))
        pl.semaphore_signal(barrier, inc=1, device_id=there, device_id_type=MESH)
        return carry

    lax.fori_loop(1, DEVS, greet, 0)

    lane = lax.broadcasted_iota(jnp.int32, (1, 128), 1)

    def place(b, carry):
        which, slot = carry
        there = dest[b]
        hit = lane == lax.div(there, BLOCKS)
        return jnp.where(hit, b, which), jnp.where(hit, lax.rem(there, BLOCKS), slot)

    load_d.wait()
    load_l.wait()
    which, slot = lax.fori_loop(
        0, BLOCKS, place, (jnp.zeros((1, 128), jnp.int32), jnp.full((1, 128), NONE, jnp.int32))
    )
    vidx[0:1, :] = which
    vidx[1:2, :] = slot
    to_smem = pltpu.make_async_copy(vidx, sidx, load_sem.at[2])
    to_smem.start()
    fill_constants(nsel, fsel, spread, tsel, weights, ax)
    to_smem.wait()


    def scale_of(b):
        level = lev[b]
        return jnp.where(level == 0, 1.0, jnp.where(level == 1, 4.0, 16.0)).astype(F32)

    def base_part(b):
        x = newest[b].reshape(48, 256)
        h0 = x.astype(F32)
        h1 = older[b, 0:3].reshape(48, 256).astype(F32)
        h2 = older[b, 3:6].reshape(48, 256).astype(F32)
        source = ((18.0 * h0 - 9.0 * h1 + 2.0 * h2) * (1.0 / 11.0)).astype(BF).astype(F32)
        c = diffusion * scale_of(b)
        radial = lax.rem(lax.broadcasted_iota(jnp.int32, (48, 256), 0), 16)
        beside = jnp.dot(x, nsel[...], preferred_element_type=F32)
        beside += jnp.where(radial == 0, 0.0, pltpu.roll(h0, 1, 0))
        beside += jnp.where(radial == 15, 0.0, pltpu.roll(h0, 47, 0))
        defect = (source - (1.0 + 6.0 * c) * h0 + c * beside).astype(BF)
        lhs = jnp.concatenate([defect[:, 0:128], defect[:, 128:256]], axis=0)
        u = lax.dot_general(lhs, tbuf[b], (((1,), (1,)), ((), ())), preferred_element_type=F32)
        return h0 + jnp.concatenate([u[0:48], u[48:96]], axis=1)

    def for_each(count, step):
        def some(n, carry):
            for k in range(UNROLL):
                step(n * UNROLL + k)
            return carry

        lax.fori_loop(0, count // UNROLL, some, 0)

    left16 = lax.broadcasted_iota(jnp.int32, (16, 128), 1) < 64
    left8 = lax.broadcasted_iota(jnp.int32, (8, 128), 1) < 64

    def pack_first(d):
        below = jnp.maximum(d - AZ, 0)
        above = jnp.minimum(d + AZ, DEVS - 1)
        slot_below = jnp.where(d >= AZ, sidx[1, below], NONE)
        slot_above = jnp.where(d < DEVS - AZ, sidx[1, above], NONE)
        meta_s[d] = jnp.where(lane < 64, sidx[1, d], slot_below * 128 + slot_above)
        own, low, high = sidx[0, d], sidx[0, below], sidx[0, above]
        faces = sum(
            jnp.dot(newest[b].reshape(48, 256), fsel[n], preferred_element_type=F32)
            for n, b in enumerate((low, high, own))
        )
        upper = jnp.where(left16, faces[0:16], faces[16:32])
        lower = jnp.where(left8, faces[32:40], faces[40:48])
        send1[d] = jnp.concatenate([upper, lower], axis=0).astype(BF)

    def columns_of(b):
        u = lax.dot_general(tsel[...], tbuf[b], (((1,), (1,)), ((), ())), preferred_element_type=F32)
        return (u * scale_of(b)).astype(BF)

    def unfold(packed):
        f = packed.astype(F32)
        parts = [f[0:16, 0:64], f[0:16, 64:128], f[16:24, 0:64], f[16:24, 64:128]]
        return jnp.concatenate(parts, axis=0).astype(BF)

    def push(src, dst, n, where):
        pltpu.make_async_remote_copy(
            src_ref=src, dst_ref=dst, send_sem=ssem.at[n], recv_sem=rsem.at[n],
            device_id=where, device_id_type=MESH,
        ).start()

    load_h0.wait()
    pl.semaphore_wait(barrier, DEVS - 1)

    def send_first(n, carry):
        targets = [target_of(ax, az, n * UNROLL + k) for k in range(UNROLL)]
        for tax, taz in targets:
            pack_first(tax * AZ + taz)
        for k, (tax, taz) in enumerate(targets):
            d = tax * AZ + taz

            def go():
                push(meta_s.at[d], meta_r.at[me], 0, (tax, taz))
                push(send1.at[d], recv1.at[me], 1, (tax, taz))

            if k > 0:
                go()
            else:
                pl.when(n > 0)(go)
        return carry

    lax.fori_loop(0, DEVS // UNROLL, send_first, 0)
    meta_r[me] = meta_s[me]
    recv1[me] = send1[me]

    load_t.wait()

    def each_target(low, high, make, go):
        def some(n, carry):
            items = [(n * UNROLL + k, target_of(ax, az, n * UNROLL + k)) for k in range(UNROLL)]
            for i, (tax, taz) in items:
                make(i, tax * AZ + taz)
            for i, (tax, taz) in items:
                go(i, tax * AZ + taz, (tax, taz))
            return carry

        lax.fori_loop(low // UNROLL, high // UNROLL, some, 0)

    def make_columns(i, d):
        send_t[i] = columns_of(sidx[0, d])

    def go_columns(i, d, where):
        pl.when(i > 0)(lambda: push(send_t.at[i], recv_t.at[me], 4, where))

    each_target(0, EARLY, make_columns, go_columns)
    recv_t[me] = send_t[0]

    def no_columns(i, carry):
        sax, saz = source_of(ax, az, i)
        recv_t[sax * AZ + saz] = jnp.zeros((48, 128), BF)
        return carry

    lax.fori_loop(EARLY, DEVS, no_columns, 0)

    load_h.wait()

    def put(d, field):
        field = field.astype(BF).reshape(3, 16, 256)
        send_a[d] = field[0:2]
        send_b[d] = field[2:3]

    def make_base(i, d):
        put(d, base_part(sidx[0, d]))

    def go_base(i, d, where):
        def go():
            push(send_a.at[d], recv_a.at[me], 2, where)
            push(send_b.at[d], recv_b.at[me], 3, where)

        pl.when(i > 0)(go)

    each_target(0, CUTS[0], make_base, go_base)
    recv_a[me] = send_a[me]
    recv_b[me] = send_b[me]

    def all_of(ref, sem, count=DEVS - 1):
        part = ref.at[pl.ds(0, count)]
        pltpu.make_async_copy(part, part, sem).wait()

    all_of(meta_r, rsem.at[0])

    def unplace(s, carry):
        mine, low, high, slot_low, slot_high = carry
        code = meta_r[s]
        mine = jnp.where(code == lane, s, mine)
        low = jnp.where(lax.div(code, 128) == lane - 64, s, low)
        high = jnp.where(lax.rem(code, 128) == lane - 64, s, high)
        slot_low = jnp.where(lane == s, code, slot_low)
        slot_high = jnp.where(lane == s - 64, code, slot_high)
        return mine, low, high, slot_low, slot_high

    def unplace_some(n, carry):
        for k in range(UNROLL):
            carry = unplace(n * UNROLL + k, carry)
        return carry

    nothing = (jnp.zeros((1, 128), jnp.int32),) * 5
    found = lax.fori_loop(0, DEVS // UNROLL, unplace_some, nothing)
    for n, row in enumerate(found):
        vinv[n : n + 1, :] = row
    to_smem = pltpu.make_async_copy(vinv, sinv, load_sem.at[2])
    to_smem.start()
    to_smem.wait()

    all_of(recv1, rsem.at[1])

    def order(j):
        ordf[j + 1] = recv1[sinv[0, j]]

    for_each(BLOCKS, order)
    edge_up = pltpu.make_async_remote_copy(
        src_ref=ordf.at[BLOCKS], dst_ref=ordf.at[0], send_sem=ssem.at[6], recv_sem=rsem.at[6],
        device_id=(ax, lax.rem(az + 1, AZ)), device_id_type=MESH,
    )
    edge_down = pltpu.make_async_remote_copy(
        src_ref=ordf.at[1], dst_ref=ordf.at[BLOCKS + 1], send_sem=ssem.at[7], recv_sem=rsem.at[7],
        device_id=(ax, lax.rem(az + AZ - 1, AZ)), device_id_type=MESH,
    )
    edge_up.start()
    edge_down.start()

    each_target(CUTS[0], CUTS[1], make_base, go_base)
    edge_up.wait_recv()
    edge_down.wait_recv()

    def gather(j):
        beside_faces[j] = (
            recv1[sinv[1, j + 64]] * weights[0]
            + recv1[sinv[2, j + 64]] * weights[1]
            + ordf[j] * weights[2]
            + ordf[j + 2] * weights[3]
        )

    for_each(BLOCKS, gather)

    def send_back(group):
        def one(i, carry):
            sax, saz = source_of(ax, az, i)
            s = sax * AZ + saz
            slot = jnp.where(s < 64, sinv[3, jnp.minimum(s, 63)], sinv[4, jnp.maximum(s - 64, 0)])
            send2[s] = beside_faces[jnp.minimum(slot, BLOCKS - 1)]
            pltpu.make_async_remote_copy(
                src_ref=send2.at[s], dst_ref=recv2.at[me], send_sem=ssem.at[5],
                recv_sem=back_sem.at[group], device_id=(sax, saz), device_id_type=MESH,
            ).start()
            return carry

        lax.fori_loop(EARLY + group * GROUP, EARLY + (group + 1) * GROUP, one, 0)

    for group in range(GROUPS):
        send_back(group)
    each_target(CUTS[1], EARLY, make_base, go_base)

    def keep_base(b):
        base[b] = base_part(b)

    for_each(BLOCKS, keep_base)

    def finish(i, d):
        b = sidx[0, d]
        nearby = jnp.dot(unfold(recv2[d]), spread[...], preferred_element_type=F32).astype(BF)
        lhs = jnp.concatenate([nearby[:, 0:128], nearby[:, 128:256]], axis=0)
        u = lax.dot_general(lhs, tbuf[b], (((1,), (1,)), ((), ())), preferred_element_type=F32)
        update = jnp.concatenate([u[0:48], u[48:96]], axis=1)
        put(d, base[b] + (diffusion * scale_of(b)) * update)

    def go_finished(i, d, where):
        push(send_a.at[d], recv_a.at[me], 2, where)

    for group in range(GROUPS):
        all_of(recv2, back_sem.at[group], GROUP)
        each_target(EARLY + group * GROUP, EARLY + (group + 1) * GROUP, finish, go_finished)

    def send_rest(i, carry):
        tax, taz = target_of(ax, az, i)
        push(send_b.at[tax * AZ + taz], recv_b.at[me], 3, (tax, taz))
        return carry

    lax.fori_loop(EARLY, DEVS, send_rest, 0)

    all_of(recv_t, rsem.at[4], EARLY - 1)

    def correct(j):
        s = sinv[0, j]
        none = jnp.zeros((16, 128), BF)
        t_low, t_high, t_side = recv_t[s, 0:16], recv_t[s, 16:32], recv_t[s, 32:48]
        rhs = jnp.concatenate(
            [
                jnp.concatenate([t_low, none, t_side, none], axis=0),
                jnp.concatenate([none, t_high, none, t_side], axis=0),
            ],
            axis=1,
        )
        update = jnp.dot(unfold(beside_faces[j]), rhs, preferred_element_type=F32) * diffusion
        stage[j] = update.reshape(3, 16, 256)

    for_each(BLOCKS, correct)

    all_of(recv_a, rsem.at[2])

    def add_a(j):
        final[j, 0:2] = (stage[j, 0:2] + recv_a[sinv[0, j]].astype(F32)).astype(BF)

    for_each(BLOCKS, add_a)
    all_of(recv_b, rsem.at[3])

    def add_b(n, carry):
        for k in range(UNROLL):
            j = n * UNROLL + k
            final[j, 2:3] = (stage[j, 2:3] + recv_b[sinv[0, j]].astype(F32)).astype(BF)
        return carry

    copies = []
    for g in range(4):
        lax.fori_loop(g * 16 // UNROLL, (g + 1) * 16 // UNROLL, add_b, 0)
        part = pl.ds(g * 16, 16)
        copies.append(pltpu.make_async_copy(final.at[part], out.at[part], out_sem.at[g]))
        copies[-1].start()

    all_of(meta_s, ssem.at[0])
    all_of(send1, ssem.at[1])
    all_of(recv_t, ssem.at[4], EARLY - 1)
    all_of(send2, ssem.at[5], DEVS - EARLY)
    all_of(send_a, ssem.at[2])
    all_of(send_b, ssem.at[3])
    edge_up.wait_send()
    edge_down.wait_send()
    for copy in copies:
        copy.wait()


def body(history, inverse_tiles, levels, destination):
    anywhere = pl.BlockSpec(memory_space=pl.ANY)
    moved = pl.pallas_call(
        kernel,
        out_shape=jax.ShapeDtypeStruct((BLOCKS, 3, 16, 256), BF),
        in_specs=[pl.BlockSpec(memory_space=pltpu.HBM)] * 4,
        out_specs=anywhere,
        scratch_shapes=[
            pltpu.VMEM((BLOCKS, 3, 16, 256), BF),
            pltpu.VMEM((BLOCKS, 6, 16, 256), BF),
            pltpu.VMEM((BLOCKS, 128, 128), BF),
            pltpu.VMEM((DEVS, 1, 128), jnp.int32),
            pltpu.VMEM((DEVS, 1, 128), jnp.int32),
            pltpu.VMEM((DEVS, FACES, 128), BF),
            pltpu.VMEM((DEVS, FACES, 128), BF),
            pltpu.VMEM((EARLY, 48, 128), BF),
            pltpu.VMEM((DEVS, 48, 128), BF),
            pltpu.VMEM((DEVS, FACES, 128), BF),
            pltpu.VMEM((DEVS, FACES, 128), BF),
            pltpu.VMEM((BLOCKS, 48, 256), F32),
            pltpu.VMEM((DEVS, 2, 16, 256), BF),
            pltpu.VMEM((DEVS, 2, 16, 256), BF),
            pltpu.VMEM((DEVS, 1, 16, 256), BF),
            pltpu.VMEM((DEVS, 1, 16, 256), BF),
            pltpu.VMEM((BLOCKS, 3, 16, 256), F32),
            pltpu.VMEM((BLOCKS, 3, 16, 256), BF),
            pltpu.VMEM((BLOCKS + 2, FACES, 128), BF),
            pltpu.VMEM((BLOCKS, FACES, 128), BF),
            pltpu.VMEM((256, 256), BF),
            pltpu.VMEM((3, 256, 128), BF),
            pltpu.VMEM((64, 256), BF),
            pltpu.VMEM((48, 128), BF),
            pltpu.VMEM((4, FACES, 128), BF),
            pltpu.SMEM((BLOCKS,), jnp.int32),
            pltpu.SMEM((BLOCKS,), jnp.int32),
            pltpu.VMEM((8, 128), jnp.int32),
            pltpu.SMEM((8, 128), jnp.int32),
            pltpu.VMEM((8, 128), jnp.int32),
            pltpu.SMEM((8, 128), jnp.int32),
            pltpu.SemaphoreType.DMA((6,)),
            pltpu.SemaphoreType.DMA((8,)),
            pltpu.SemaphoreType.DMA((8,)),
            pltpu.SemaphoreType.DMA((GROUPS,)),
            pltpu.SemaphoreType.DMA((4,)),
        ],
        compiler_params=pltpu.CompilerParams(
            collective_id=0, has_side_effects=True, vmem_limit_bytes=60 * 2**20
        ),
    )(history.reshape(BLOCKS, 9, 16, 256), inverse_tiles, destination, levels)
    return moved.astype(F32)


def solution(mesh):
    placed = (
        P(("ax", "az"), None, None, None, None),
        P(("ax", "az"), None, None),
        P(("ax", "az")),
        P(("ax", "az")),
    )
    return jax.shard_map(
        body,
        mesh=mesh,
        in_specs=placed,
        out_specs=P(("ax", "az"), None, None, None),
        check_vma=False,
    )
```

```python
import functools

import jax
import jax.numpy as jnp
from jax import lax
from jax.experimental import pallas as pl
from jax.experimental.pallas import tpu as pltpu
from jax.sharding import PartitionSpec as P

diffusion = 0.04
MESH = pl.DeviceIdType.MESH
F32 = jnp.float32
BF = jnp.bfloat16

BLOCKS = 64
DEVS = 128
AZ = 8
FACES = 24
EARLY = 44
STRIDE = 107
UNROLL = 4
CUTS = (4, 16)
GROUPS = 3
GROUP = (DEVS - EARLY) // GROUPS
PARTS = 4
NONE = 127


def target_of(ax, az, i):
    o = lax.rem(i * STRIDE, DEVS)
    dc = lax.rem(o, 2)
    dy = lax.rem(lax.div(o, 2), 4)
    dx = lax.rem(lax.div(o, 8), 4)
    dz = lax.div(o, 32)
    z = lax.rem(lax.div(ax, 4) + dz, 4)
    x = lax.rem(lax.rem(ax, 4) + dx, 4)
    y = lax.rem(lax.div(az, 2) + dy, 4)
    c = lax.rem(lax.rem(az, 2) + dc, 2)
    return z * 4 + x, y * 2 + c


def source_of(ax, az, i):
    o = lax.rem(i * STRIDE, DEVS)
    dc = lax.rem(o, 2)
    dy = lax.rem(lax.div(o, 2), 4)
    dx = lax.rem(lax.div(o, 8), 4)
    dz = lax.div(o, 32)
    z = lax.rem(lax.div(ax, 4) - dz + 4, 4)
    x = lax.rem(lax.rem(ax, 4) - dx + 4, 4)
    y = lax.rem(lax.div(az, 2) - dy + 4, 4)
    c = lax.rem(lax.rem(az, 2) - dc + 2, 2)
    return z * 4 + x, y * 2 + c


def bf16_of(mask):
    return jnp.where(mask, 1.0, 0.0).astype(BF)


def fill_constants(nsel, fsel, spread, tsel, weights, ax):
    src = lax.broadcasted_iota(jnp.int32, (256, 256), 0)
    dst = lax.broadcasted_iota(jnp.int32, (256, 256), 1)
    ps, qs = lax.div(src, 16), lax.rem(src, 16)
    pd, qd = lax.div(dst, 16), lax.rem(dst, 16)
    beside = ((ps == pd) & (jnp.abs(qs - qd) == 1)) | ((qs == qd) & (jnp.abs(ps - pd) == 1))
    nsel[...] = bf16_of(beside)
    src = lax.broadcasted_iota(jnp.int32, (256, 128), 0)
    kk = lax.rem(lax.broadcasted_iota(jnp.int32, (256, 128), 1), 64)
    plane = jnp.where(kk < 48, 0, 8) + lax.rem(kk, 8)
    pick = jnp.where(
        kk < 16,
        240 + kk,
        jnp.where(kk < 32, kk - 16, plane * 16 + jnp.where(lax.rem(kk, 16) < 8, 15, 0)),
    )
    low, high = kk < 16, (kk >= 16) & (kk < 32)
    fsel[0] = bf16_of((src == pick) & low)
    fsel[1] = bf16_of((src == pick) & high)
    fsel[2] = bf16_of((src == pick) & (kk >= 32))
    row = lax.broadcasted_iota(jnp.int32, (48, 128), 0)
    col = lax.broadcasted_iota(jnp.int32, (48, 128), 1)
    pick = jnp.where(
        row < 16,
        row,
        jnp.where(row < 32, 96 + row, lax.rem(row, 8) * 16 + jnp.where(row < 40, 0, 15)),
    )
    tsel[...] = bf16_of(col == pick)
    kk = lax.broadcasted_iota(jnp.int32, (64, 256), 0)
    dst = lax.broadcasted_iota(jnp.int32, (64, 256), 1)
    plane = jnp.where(kk < 48, 0, 8) + lax.rem(kk, 8)
    pick = jnp.where(
        kk < 16,
        kk,
        jnp.where(kk < 32, 224 + kk, plane * 16 + jnp.where(lax.rem(kk, 16) < 8, 0, 15)),
    )
    spread[...] = bf16_of(dst == pick)
    kk = lax.rem(lax.broadcasted_iota(jnp.int32, (FACES, 128), 1), 64)
    weights[0] = bf16_of((kk < 16) & (ax > 0))
    weights[1] = bf16_of((kk >= 16) & (kk < 32) & (ax < 15))
    weights[2] = bf16_of((kk >= 32) & (lax.rem(kk, 16) < 8))
    weights[3] = bf16_of((kk >= 32) & (lax.rem(kk, 16) >= 8))


def kernel(
    hist, tiles, dest_any, lev_any, out,
    newest, older, tbuf, meta_s, meta_r, send1, recv1, send_t, recv_t, send2, recv2,
    send_a, recv_a, send_b, recv_b, stage, final, ordf, beside_faces,
    nsel, fsel, spread, tsel, weights, dest, lev, vidx, sidx, vinv, sinv,
    load_sem, ssem, rsem, back_sem, out_sem,
):
    ax = lax.axis_index("ax")
    az = lax.axis_index("az")
    me = ax * AZ + az
    barrier = pltpu.get_barrier_semaphore()

    load_d = pltpu.make_async_copy(dest_any, dest, load_sem.at[3])
    load_l = pltpu.make_async_copy(lev_any, lev, load_sem.at[4])
    load_h0 = pltpu.make_async_copy(hist.at[:, pl.ds(0, 3)], newest, load_sem.at[0])
    load_h = pltpu.make_async_copy(hist.at[:, pl.ds(3, 6)], older, load_sem.at[5])
    load_t = pltpu.make_async_copy(tiles, tbuf, load_sem.at[1])
    loads = (load_d, load_l, load_h0, load_t, load_h)
    for load in loads:
        load.start()

    def greet(i, carry):
        t = lax.rem(me + i, DEVS)
        there = (lax.div(t, AZ), lax.rem(t, AZ))
        pl.semaphore_signal(barrier, inc=1, device_id=there, device_id_type=MESH)
        return carry

    lax.fori_loop(1, DEVS, greet, 0)

    lane = lax.broadcasted_iota(jnp.int32, (1, 128), 1)

    def place(b, carry):
        which, slot = carry
        there = dest[b]
        hit = lane == lax.div(there, BLOCKS)
        return jnp.where(hit, b, which), jnp.where(hit, lax.rem(there, BLOCKS), slot)

    load_d.wait()
    load_l.wait()
    which, slot = lax.fori_loop(
        0, BLOCKS, place, (jnp.zeros((1, 128), jnp.int32), jnp.full((1, 128), NONE, jnp.int32))
    )
    vidx[0:1, :] = which
    vidx[1:2, :] = slot
    to_smem = pltpu.make_async_copy(vidx, sidx, load_sem.at[2])
    to_smem.start()
    fill_constants(nsel, fsel, spread, tsel, weights, ax)
    to_smem.wait()


    def scale_of(b):
        level = lev[b]
        return jnp.where(level == 0, 1.0, jnp.where(level == 1, 4.0, 16.0)).astype(F32)

    def swept(b, nearby=None):
        x = newest[b].reshape(48, 256)
        h0 = x.astype(F32)
        h1 = older[b, 0:3].reshape(48, 256).astype(F32)
        h2 = older[b, 3:6].reshape(48, 256).astype(F32)
        source = ((18.0 * h0 - 9.0 * h1 + 2.0 * h2) * (1.0 / 11.0)).astype(BF).astype(F32)
        c = diffusion * scale_of(b)
        radial = lax.rem(lax.broadcasted_iota(jnp.int32, (48, 256), 0), 16)
        beside = jnp.dot(x, nsel[...], preferred_element_type=F32)
        beside += jnp.where(radial == 0, 0.0, pltpu.roll(h0, 1, 0))
        beside += jnp.where(radial == 15, 0.0, pltpu.roll(h0, 47, 0))
        if nearby is not None:
            beside += nearby
        defect = (source - (1.0 + 6.0 * c) * h0 + c * beside).astype(BF)
        lhs = jnp.concatenate([defect[:, 0:128], defect[:, 128:256]], axis=0)
        u = lax.dot_general(lhs, tbuf[b], (((1,), (1,)), ((), ())), preferred_element_type=F32)
        return h0 + jnp.concatenate([u[0:48], u[48:96]], axis=1)

    def for_each(count, step):
        def some(n, carry):
            for k in range(UNROLL):
                step(n * UNROLL + k)
            return carry

        lax.fori_loop(0, count // UNROLL, some, 0)

    left16 = lax.broadcasted_iota(jnp.int32, (16, 128), 1) < 64
    left8 = lax.broadcasted_iota(jnp.int32, (8, 128), 1) < 64

    def pack_first(d):
        below = jnp.maximum(d - AZ, 0)
        above = jnp.minimum(d + AZ, DEVS - 1)
        slot_below = jnp.where(d >= AZ, sidx[1, below], NONE)
        slot_above = jnp.where(d < DEVS - AZ, sidx[1, above], NONE)
        meta_s[d] = jnp.where(lane < 64, sidx[1, d], slot_below * 128 + slot_above)
        own, low, high = sidx[0, d], sidx[0, below], sidx[0, above]
        faces = sum(
            jnp.dot(newest[b].reshape(48, 256), fsel[n], preferred_element_type=F32)
            for n, b in enumerate((low, high, own))
        )
        upper = jnp.where(left16, faces[0:16], faces[16:32])
        lower = jnp.where(left8, faces[32:40], faces[40:48])
        send1[d] = jnp.concatenate([upper, lower], axis=0).astype(BF)

    def columns_of(b):
        u = lax.dot_general(tsel[...], tbuf[b], (((1,), (1,)), ((), ())), preferred_element_type=F32)
        return (u * scale_of(b)).astype(BF)

    def unfold(packed):
        f = packed.astype(F32)
        parts = [f[0:16, 0:64], f[0:16, 64:128], f[16:24, 0:64], f[16:24, 64:128]]
        return jnp.concatenate(parts, axis=0).astype(BF)

    def push(src, dst, n, where):
        pltpu.make_async_remote_copy(
            src_ref=src, dst_ref=dst, send_sem=ssem.at[n], recv_sem=rsem.at[n],
            device_id=where, device_id_type=MESH,
        ).start()

    load_h0.wait()
    pl.semaphore_wait(barrier, DEVS - 1)

    def send_first(n, carry):
        targets = [target_of(ax, az, n * UNROLL + k) for k in range(UNROLL)]
        for tax, taz in targets:
            pack_first(tax * AZ + taz)
        for k, (tax, taz) in enumerate(targets):
            d = tax * AZ + taz

            def go():
                push(meta_s.at[d], meta_r.at[me], 0, (tax, taz))
                push(send1.at[d], recv1.at[me], 1, (tax, taz))

            if k > 0:
                go()
            else:
                pl.when(n > 0)(go)
        return carry

    lax.fori_loop(0, DEVS // UNROLL, send_first, 0)
    meta_r[me] = meta_s[me]
    recv1[me] = send1[me]

    load_t.wait()

    def each_target(low, high, make, go):
        def some(n, carry):
            items = [(n * UNROLL + k, target_of(ax, az, n * UNROLL + k)) for k in range(UNROLL)]
            for i, (tax, taz) in items:
                make(i, tax * AZ + taz)
            for i, (tax, taz) in items:
                go(i, tax * AZ + taz, (tax, taz))
            return carry

        lax.fori_loop(low // UNROLL, high // UNROLL, some, 0)

    def make_columns(i, d):
        send_t[i] = columns_of(sidx[0, d])

    def go_columns(i, d, where):
        pl.when(i > 0)(lambda: push(send_t.at[i], recv_t.at[me], 4, where))

    each_target(0, EARLY, make_columns, go_columns)
    recv_t[me] = send_t[0]

    def no_columns(i, carry):
        sax, saz = source_of(ax, az, i)
        recv_t[sax * AZ + saz] = jnp.zeros((48, 128), BF)
        return carry

    lax.fori_loop(EARLY, DEVS, no_columns, 0)

    load_h.wait()

    def put(d, field):
        field = field.astype(BF).reshape(3, 16, 256)
        send_a[d] = field[0:2]
        send_b[d] = field[2:3]

    def make_base(i, d):
        put(d, swept(sidx[0, d]))

    def go_base(i, d, where):
        def go():
            push(send_a.at[d], recv_a.at[me], 2, where)
            push(send_b.at[d], recv_b.at[me], 3, where)

        pl.when(i > 0)(go)

    each_target(0, CUTS[0], make_base, go_base)
    recv_a[me] = send_a[me]
    recv_b[me] = send_b[me]

    def all_of(ref, sem, count=DEVS - 1):
        part = ref.at[pl.ds(0, count)]
        pltpu.make_async_copy(part, part, sem).wait()

    all_of(meta_r, rsem.at[0])

    def unplace(s, carry):
        mine, low, high, slot_low, slot_high = carry
        code = meta_r[s]
        mine = jnp.where(code == lane, s, mine)
        low = jnp.where(lax.div(code, 128) == lane - 64, s, low)
        high = jnp.where(lax.rem(code, 128) == lane - 64, s, high)
        slot_low = jnp.where(lane == s, code, slot_low)
        slot_high = jnp.where(lane == s - 64, code, slot_high)
        return mine, low, high, slot_low, slot_high

    def unplace_some(n, carry):
        for k in range(UNROLL):
            carry = unplace(n * UNROLL + k, carry)
        return carry

    nothing = (jnp.zeros((1, 128), jnp.int32),) * 5
    found = lax.fori_loop(0, DEVS // UNROLL, unplace_some, nothing)
    for n, row in enumerate(found):
        vinv[n : n + 1, :] = row
    to_smem = pltpu.make_async_copy(vinv, sinv, load_sem.at[2])
    to_smem.start()
    to_smem.wait()

    all_of(recv1, rsem.at[1])

    def order(j):
        ordf[j + 1] = recv1[sinv[0, j]]

    for_each(BLOCKS, order)
    edge_up = pltpu.make_async_remote_copy(
        src_ref=ordf.at[BLOCKS], dst_ref=ordf.at[0], send_sem=ssem.at[6], recv_sem=rsem.at[6],
        device_id=(ax, lax.rem(az + 1, AZ)), device_id_type=MESH,
    )
    edge_down = pltpu.make_async_remote_copy(
        src_ref=ordf.at[1], dst_ref=ordf.at[BLOCKS + 1], send_sem=ssem.at[7], recv_sem=rsem.at[7],
        device_id=(ax, lax.rem(az + AZ - 1, AZ)), device_id_type=MESH,
    )
    edge_up.start()
    edge_down.start()

    each_target(CUTS[0], CUTS[1], make_base, go_base)
    edge_up.wait_recv()
    edge_down.wait_recv()

    def gather(j):
        beside_faces[j] = (
            recv1[sinv[1, j + 64]] * weights[0]
            + recv1[sinv[2, j + 64]] * weights[1]
            + ordf[j] * weights[2]
            + ordf[j + 2] * weights[3]
        )

    for_each(BLOCKS, gather)

    def send_back(group):
        def one(i, carry):
            sax, saz = source_of(ax, az, i)
            s = sax * AZ + saz
            slot = jnp.where(s < 64, sinv[3, jnp.minimum(s, 63)], sinv[4, jnp.maximum(s - 64, 0)])
            send2[s] = beside_faces[jnp.minimum(slot, BLOCKS - 1)]
            pltpu.make_async_remote_copy(
                src_ref=send2.at[s], dst_ref=recv2.at[me], send_sem=ssem.at[5],
                recv_sem=back_sem.at[group], device_id=(sax, saz), device_id_type=MESH,
            ).start()
            return carry

        lax.fori_loop(EARLY + group * GROUP, EARLY + (group + 1) * GROUP, one, 0)

    for group in range(GROUPS):
        send_back(group)
    each_target(CUTS[1], EARLY, make_base, go_base)

    def finish(i, d):
        nearby = jnp.dot(unfold(recv2[d]), spread[...], preferred_element_type=F32)
        put(d, swept(sidx[0, d], nearby))

    def go_whole(i, d, where):
        push(send_a.at[d], recv_a.at[me], 2, where)
        push(send_b.at[d], recv_b.at[me], 3, where)

    def go_first(i, d, where):
        push(send_a.at[d], recv_a.at[me], 2, where)

    for group in range(GROUPS):
        all_of(recv2, back_sem.at[group], GROUP)
        each_target(EARLY + group * GROUP, EARLY + (group + 1) * GROUP, finish, go_whole if group < GROUPS - 1 else go_first)

    def send_rest(i, carry):
        tax, taz = target_of(ax, az, i)
        push(send_b.at[tax * AZ + taz], recv_b.at[me], 3, (tax, taz))
        return carry

    lax.fori_loop(DEVS - GROUP, DEVS, send_rest, 0)

    all_of(recv_t, rsem.at[4], EARLY - 1)

    def correct(j):
        s = sinv[0, j]
        none = jnp.zeros((16, 128), BF)
        t_low, t_high, t_side = recv_t[s, 0:16], recv_t[s, 16:32], recv_t[s, 32:48]
        rhs = jnp.concatenate(
            [
                jnp.concatenate([t_low, none, t_side, none], axis=0),
                jnp.concatenate([none, t_high, none, t_side], axis=0),
            ],
            axis=1,
        )
        update = jnp.dot(unfold(beside_faces[j]), rhs, preferred_element_type=F32) * diffusion
        stage[j] = update.reshape(3, 16, 256)

    for_each(BLOCKS, correct)

    all_of(recv_a, rsem.at[2])

    def add_a(j):
        final[j, 0:2] = (stage[j, 0:2] + recv_a[sinv[0, j]].astype(F32)).astype(BF)

    for_each(BLOCKS, add_a)
    all_of(recv_b, rsem.at[3])

    def add_b(n, carry):
        for k in range(UNROLL):
            j = n * UNROLL + k
            final[j, 2:3] = (stage[j, 2:3] + recv_b[sinv[0, j]].astype(F32)).astype(BF)
        return carry

    copies = []
    for g in range(4):
        lax.fori_loop(g * 16 // UNROLL, (g + 1) * 16 // UNROLL, add_b, 0)
        part = pl.ds(g * 16, 16)
        copies.append(pltpu.make_async_copy(final.at[part], out.at[part], out_sem.at[g]))
        copies[-1].start()

    all_of(meta_s, ssem.at[0])
    all_of(send1, ssem.at[1])
    all_of(recv_t, ssem.at[4], EARLY - 1)
    all_of(send2, ssem.at[5], DEVS - EARLY)
    all_of(send_a, ssem.at[2])
    all_of(send_b, ssem.at[3])
    edge_up.wait_send()
    edge_down.wait_send()
    for copy in copies:
        copy.wait()


def widen(narrow, wide, held, widened, in_sem, out_sem):
    size = BLOCKS // PARTS
    parts = [pl.ds(n * size, size) for n in range(PARTS)]
    loads = [pltpu.make_async_copy(narrow.at[p], held.at[p], in_sem.at[n]) for n, p in enumerate(parts)]
    stores = [pltpu.make_async_copy(widened.at[p], wide.at[p], out_sem.at[n]) for n, p in enumerate(parts)]
    for load in loads:
        load.start()
    for n in range(PARTS):
        loads[n].wait()

        def one(j, carry):
            for k in range(UNROLL):
                b = n * size + j * UNROLL + k
                widened[b] = held[b].astype(F32)
            return carry

        lax.fori_loop(0, size // UNROLL, one, 0)
        stores[n].start()
    for store in stores:
        store.wait()


def body(history, inverse_tiles, levels, destination):
    anywhere = pl.BlockSpec(memory_space=pl.ANY)
    moved = pl.pallas_call(
        kernel,
        out_shape=jax.ShapeDtypeStruct((BLOCKS, 3, 16, 256), BF),
        in_specs=[pl.BlockSpec(memory_space=pltpu.HBM)] * 4,
        out_specs=anywhere,
        scratch_shapes=[
            pltpu.VMEM((BLOCKS, 3, 16, 256), BF),
            pltpu.VMEM((BLOCKS, 6, 16, 256), BF),
            pltpu.VMEM((BLOCKS, 128, 128), BF),
            pltpu.VMEM((DEVS, 1, 128), jnp.int32),
            pltpu.VMEM((DEVS, 1, 128), jnp.int32),
            pltpu.VMEM((DEVS, FACES, 128), BF),
            pltpu.VMEM((DEVS, FACES, 128), BF),
            pltpu.VMEM((EARLY, 48, 128), BF),
            pltpu.VMEM((DEVS, 48, 128), BF),
            pltpu.VMEM((DEVS, FACES, 128), BF),
            pltpu.VMEM((DEVS, FACES, 128), BF),
            pltpu.VMEM((DEVS, 2, 16, 256), BF),
            pltpu.VMEM((DEVS, 2, 16, 256), BF),
            pltpu.VMEM((DEVS, 1, 16, 256), BF),
            pltpu.VMEM((DEVS, 1, 16, 256), BF),
            pltpu.VMEM((BLOCKS, 3, 16, 256), F32),
            pltpu.VMEM((BLOCKS, 3, 16, 256), BF),
            pltpu.VMEM((BLOCKS + 2, FACES, 128), BF),
            pltpu.VMEM((BLOCKS, FACES, 128), BF),
            pltpu.VMEM((256, 256), BF),
            pltpu.VMEM((3, 256, 128), BF),
            pltpu.VMEM((64, 256), BF),
            pltpu.VMEM((48, 128), BF),
            pltpu.VMEM((4, FACES, 128), BF),
            pltpu.SMEM((BLOCKS,), jnp.int32),
            pltpu.SMEM((BLOCKS,), jnp.int32),
            pltpu.VMEM((8, 128), jnp.int32),
            pltpu.SMEM((8, 128), jnp.int32),
            pltpu.VMEM((8, 128), jnp.int32),
            pltpu.SMEM((8, 128), jnp.int32),
            pltpu.SemaphoreType.DMA((6,)),
            pltpu.SemaphoreType.DMA((8,)),
            pltpu.SemaphoreType.DMA((8,)),
            pltpu.SemaphoreType.DMA((GROUPS,)),
            pltpu.SemaphoreType.DMA((4,)),
        ],
        compiler_params=pltpu.CompilerParams(
            collective_id=0, has_side_effects=True, vmem_limit_bytes=60 * 2**20
        ),
    )(history.reshape(BLOCKS, 9, 16, 256), inverse_tiles, destination, levels)
    return pl.pallas_call(
        widen,
        out_shape=jax.ShapeDtypeStruct((BLOCKS, 3, 16, 256), F32),
        in_specs=[pl.BlockSpec(memory_space=pltpu.HBM)],
        out_specs=pl.BlockSpec(memory_space=pltpu.HBM),
        scratch_shapes=[
            pltpu.VMEM((BLOCKS, 3, 16, 256), BF),
            pltpu.VMEM((BLOCKS, 3, 16, 256), F32),
            pltpu.SemaphoreType.DMA((PARTS,)),
            pltpu.SemaphoreType.DMA((PARTS,)),
        ],
        compiler_params=pltpu.CompilerParams(vmem_limit_bytes=60 * 2**20),
    )(moved)


def solution(mesh):
    placed = (
        P(("ax", "az"), None, None, None, None),
        P(("ax", "az"), None, None),
        P(("ax", "az")),
        P(("ax", "az")),
    )
    return jax.shard_map(
        body,
        mesh=mesh,
        in_specs=placed,
        out_specs=P(("ax", "az"), None, None, None),
        check_vma=False,
    )
```

```python
import functools

import jax
import jax.numpy as jnp
from jax import lax
from jax.experimental import pallas as pl
from jax.experimental.pallas import tpu as pltpu
from jax.sharding import PartitionSpec as P

diffusion = 0.04
MESH = pl.DeviceIdType.MESH
F32 = jnp.float32
BF = jnp.bfloat16

BLOCKS = 64
DEVS = 128
AZ = 8
FACES = 24
EARLY = 44
STRIDE = 81
UNROLL = 4
CUTS = (8, 24)
GROUPS = 3
GROUP = (DEVS - EARLY) // GROUPS
PARTS = 4
NONE = 127


def target_of(ax, az, i):
    o = lax.rem(i * STRIDE, DEVS)
    dc = lax.rem(o, 2)
    dy = lax.rem(lax.div(o, 2), 4)
    dx = lax.rem(lax.div(o, 8), 4)
    dz = lax.div(o, 32)
    z = lax.rem(lax.div(ax, 4) + dz, 4)
    x = lax.rem(lax.rem(ax, 4) + dx, 4)
    y = lax.rem(lax.div(az, 2) + dy, 4)
    c = lax.rem(lax.rem(az, 2) + dc, 2)
    return z * 4 + x, y * 2 + c


def source_of(ax, az, i):
    o = lax.rem(i * STRIDE, DEVS)
    dc = lax.rem(o, 2)
    dy = lax.rem(lax.div(o, 2), 4)
    dx = lax.rem(lax.div(o, 8), 4)
    dz = lax.div(o, 32)
    z = lax.rem(lax.div(ax, 4) - dz + 4, 4)
    x = lax.rem(lax.rem(ax, 4) - dx + 4, 4)
    y = lax.rem(lax.div(az, 2) - dy + 4, 4)
    c = lax.rem(lax.rem(az, 2) - dc + 2, 2)
    return z * 4 + x, y * 2 + c


def bf16_of(mask):
    return jnp.where(mask, 1.0, 0.0).astype(BF)


def fill_constants(nsel, fsel, spread, tsel, weights, ax):
    src = lax.broadcasted_iota(jnp.int32, (256, 256), 0)
    dst = lax.broadcasted_iota(jnp.int32, (256, 256), 1)
    ps, qs = lax.div(src, 16), lax.rem(src, 16)
    pd, qd = lax.div(dst, 16), lax.rem(dst, 16)
    beside = ((ps == pd) & (jnp.abs(qs - qd) == 1)) | ((qs == qd) & (jnp.abs(ps - pd) == 1))
    nsel[...] = bf16_of(beside)
    src = lax.broadcasted_iota(jnp.int32, (256, 128), 0)
    kk = lax.rem(lax.broadcasted_iota(jnp.int32, (256, 128), 1), 64)
    plane = jnp.where(kk < 48, 0, 8) + lax.rem(kk, 8)
    pick = jnp.where(
        kk < 16,
        240 + kk,
        jnp.where(kk < 32, kk - 16, plane * 16 + jnp.where(lax.rem(kk, 16) < 8, 15, 0)),
    )
    low, high = kk < 16, (kk >= 16) & (kk < 32)
    fsel[0] = bf16_of((src == pick) & low)
    fsel[1] = bf16_of((src == pick) & high)
    fsel[2] = bf16_of((src == pick) & (kk >= 32))
    row = lax.broadcasted_iota(jnp.int32, (48, 128), 0)
    col = lax.broadcasted_iota(jnp.int32, (48, 128), 1)
    pick = jnp.where(
        row < 16,
        row,
        jnp.where(row < 32, 96 + row, lax.rem(row, 8) * 16 + jnp.where(row < 40, 0, 15)),
    )
    tsel[...] = bf16_of(col == pick)
    kk = lax.broadcasted_iota(jnp.int32, (64, 256), 0)
    dst = lax.broadcasted_iota(jnp.int32, (64, 256), 1)
    plane = jnp.where(kk < 48, 0, 8) + lax.rem(kk, 8)
    pick = jnp.where(
        kk < 16,
        kk,
        jnp.where(kk < 32, 224 + kk, plane * 16 + jnp.where(lax.rem(kk, 16) < 8, 0, 15)),
    )
    spread[...] = bf16_of(dst == pick)
    kk = lax.rem(lax.broadcasted_iota(jnp.int32, (FACES, 128), 1), 64)
    weights[0] = bf16_of((kk < 16) & (ax > 0))
    weights[1] = bf16_of((kk >= 16) & (kk < 32) & (ax < 15))
    weights[2] = bf16_of((kk >= 32) & (lax.rem(kk, 16) < 8))
    weights[3] = bf16_of((kk >= 32) & (lax.rem(kk, 16) >= 8))


def kernel(
    hist, tiles, dest_any, lev_any, out,
    newest, older, tbuf, meta_s, meta_r, send1, recv1, send_t, recv_t, send2, recv2,
    send_a, recv_a, send_b, recv_b, stage, final, ordf, beside_faces,
    nsel, fsel, spread, tsel, weights, dest, lev, vidx, sidx, vinv, sinv,
    load_sem, ssem, rsem, back_sem, out_sem,
):
    ax = lax.axis_index("ax")
    az = lax.axis_index("az")
    me = ax * AZ + az
    barrier = pltpu.get_barrier_semaphore()

    load_d = pltpu.make_async_copy(dest_any, dest, load_sem.at[3])
    load_l = pltpu.make_async_copy(lev_any, lev, load_sem.at[4])
    load_h0 = pltpu.make_async_copy(hist.at[:, pl.ds(0, 3)], newest, load_sem.at[0])
    load_h = pltpu.make_async_copy(hist.at[:, pl.ds(3, 6)], older, load_sem.at[5])
    load_t = pltpu.make_async_copy(tiles, tbuf, load_sem.at[1])
    loads = (load_d, load_l, load_h0, load_t, load_h)
    for load in loads:
        load.start()

    def greet(i, carry):
        t = lax.rem(me + i, DEVS)
        there = (lax.div(t, AZ), lax.rem(t, AZ))
        pl.semaphore_signal(barrier, inc=1, device_id=there, device_id_type=MESH)
        return carry

    lax.fori_loop(1, DEVS, greet, 0)

    lane = lax.broadcasted_iota(jnp.int32, (1, 128), 1)

    def place(b, carry):
        which, slot = carry
        there = dest[b]
        hit = lane == lax.div(there, BLOCKS)
        return jnp.where(hit, b, which), jnp.where(hit, lax.rem(there, BLOCKS), slot)

    load_d.wait()
    load_l.wait()
    which, slot = lax.fori_loop(
        0, BLOCKS, place, (jnp.zeros((1, 128), jnp.int32), jnp.full((1, 128), NONE, jnp.int32))
    )
    vidx[0:1, :] = which
    vidx[1:2, :] = slot
    to_smem = pltpu.make_async_copy(vidx, sidx, load_sem.at[2])
    to_smem.start()
    fill_constants(nsel, fsel, spread, tsel, weights, ax)
    to_smem.wait()


    def scale_of(b):
        level = lev[b]
        return jnp.where(level == 0, 1.0, jnp.where(level == 1, 4.0, 16.0)).astype(F32)

    def swept(b, nearby=None):
        x = newest[b].reshape(48, 256)
        h0 = x.astype(F32)
        h1 = older[b, 0:3].reshape(48, 256).astype(F32)
        h2 = older[b, 3:6].reshape(48, 256).astype(F32)
        source = ((18.0 * h0 - 9.0 * h1 + 2.0 * h2) * (1.0 / 11.0)).astype(BF).astype(F32)
        c = diffusion * scale_of(b)
        radial = lax.rem(lax.broadcasted_iota(jnp.int32, (48, 256), 0), 16)
        beside = jnp.dot(x, nsel[...], preferred_element_type=F32)
        beside += jnp.where(radial == 0, 0.0, pltpu.roll(h0, 1, 0))
        beside += jnp.where(radial == 15, 0.0, pltpu.roll(h0, 47, 0))
        if nearby is not None:
            beside += nearby
        defect = (source - (1.0 + 6.0 * c) * h0 + c * beside).astype(BF)
        lhs = jnp.concatenate([defect[:, 0:128], defect[:, 128:256]], axis=0)
        u = lax.dot_general(lhs, tbuf[b], (((1,), (1,)), ((), ())), preferred_element_type=F32)
        return h0 + jnp.concatenate([u[0:48], u[48:96]], axis=1)

    def for_each(count, step):
        def some(n, carry):
            for k in range(UNROLL):
                step(n * UNROLL + k)
            return carry

        lax.fori_loop(0, count // UNROLL, some, 0)

    left16 = lax.broadcasted_iota(jnp.int32, (16, 128), 1) < 64
    left8 = lax.broadcasted_iota(jnp.int32, (8, 128), 1) < 64

    def pack_first(d):
        below = jnp.maximum(d - AZ, 0)
        above = jnp.minimum(d + AZ, DEVS - 1)
        slot_below = jnp.where(d >= AZ, sidx[1, below], NONE)
        slot_above = jnp.where(d < DEVS - AZ, sidx[1, above], NONE)
        meta_s[d] = jnp.where(lane < 64, sidx[1, d], slot_below * 128 + slot_above)
        own, low, high = sidx[0, d], sidx[0, below], sidx[0, above]
        faces = sum(
            jnp.dot(newest[b].reshape(48, 256), fsel[n], preferred_element_type=F32)
            for n, b in enumerate((low, high, own))
        )
        upper = jnp.where(left16, faces[0:16], faces[16:32])
        lower = jnp.where(left8, faces[32:40], faces[40:48])
        send1[d] = jnp.concatenate([upper, lower], axis=0).astype(BF)

    def columns_of(b):
        u = lax.dot_general(tsel[...], tbuf[b], (((1,), (1,)), ((), ())), preferred_element_type=F32)
        return (u * scale_of(b)).astype(BF)

    def unfold(packed):
        f = packed.astype(F32)
        parts = [f[0:16, 0:64], f[0:16, 64:128], f[16:24, 0:64], f[16:24, 64:128]]
        return jnp.concatenate(parts, axis=0).astype(BF)

    def push(src, dst, n, where):
        pltpu.make_async_remote_copy(
            src_ref=src, dst_ref=dst, send_sem=ssem.at[n], recv_sem=rsem.at[n],
            device_id=where, device_id_type=MESH,
        ).start()

    load_h0.wait()
    pl.semaphore_wait(barrier, DEVS - 1)

    def send_first(n, carry):
        targets = [target_of(ax, az, n * UNROLL + k) for k in range(UNROLL)]
        for tax, taz in targets:
            pack_first(tax * AZ + taz)
        for k, (tax, taz) in enumerate(targets):
            d = tax * AZ + taz

            def go():
                push(meta_s.at[d], meta_r.at[me], 0, (tax, taz))
                push(send1.at[d], recv1.at[me], 1, (tax, taz))

            if k > 0:
                go()
            else:
                pl.when(n > 0)(go)
        return carry

    lax.fori_loop(0, DEVS // UNROLL, send_first, 0)
    meta_r[me] = meta_s[me]
    recv1[me] = send1[me]

    load_t.wait()

    def each_target(low, high, make, go):
        def some(n, carry):
            items = [(n * UNROLL + k, target_of(ax, az, n * UNROLL + k)) for k in range(UNROLL)]
            for i, (tax, taz) in items:
                make(i, tax * AZ + taz)
            for i, (tax, taz) in items:
                go(i, tax * AZ + taz, (tax, taz))
            return carry

        lax.fori_loop(low // UNROLL, high // UNROLL, some, 0)

    def make_columns(i, d):
        send_t[i] = columns_of(sidx[0, d])

    def go_columns(i, d, where):
        pl.when(i > 0)(lambda: push(send_t.at[i], recv_t.at[me], 4, where))

    each_target(0, EARLY, make_columns, go_columns)
    recv_t[me] = send_t[0]

    def no_columns(i, carry):
        sax, saz = source_of(ax, az, i)
        recv_t[sax * AZ + saz] = jnp.zeros((48, 128), BF)
        return carry

    lax.fori_loop(EARLY, DEVS, no_columns, 0)

    load_h.wait()

    def put(d, field):
        field = field.astype(BF).reshape(3, 16, 256)
        send_a[d] = field[0:2]
        send_b[d] = field[2:3]

    def make_base(i, d):
        put(d, swept(sidx[0, d]))

    def go_base(i, d, where):
        def go():
            push(send_a.at[d], recv_a.at[me], 2, where)
            push(send_b.at[d], recv_b.at[me], 3, where)

        pl.when(i > 0)(go)

    each_target(0, CUTS[0], make_base, go_base)
    recv_a[me] = send_a[me]
    recv_b[me] = send_b[me]

    def all_of(ref, sem, count=DEVS - 1):
        part = ref.at[pl.ds(0, count)]
        pltpu.make_async_copy(part, part, sem).wait()

    all_of(meta_r, rsem.at[0])

    def unplace(s, carry):
        mine, low, high, slot_low, slot_high = carry
        code = meta_r[s]
        mine = jnp.where(code == lane, s, mine)
        low = jnp.where(lax.div(code, 128) == lane - 64, s, low)
        high = jnp.where(lax.rem(code, 128) == lane - 64, s, high)
        slot_low = jnp.where(lane == s, code, slot_low)
        slot_high = jnp.where(lane == s - 64, code, slot_high)
        return mine, low, high, slot_low, slot_high

    def unplace_some(n, carry):
        for k in range(UNROLL):
            carry = unplace(n * UNROLL + k, carry)
        return carry

    nothing = (jnp.zeros((1, 128), jnp.int32),) * 5
    found = lax.fori_loop(0, DEVS // UNROLL, unplace_some, nothing)
    for n, row in enumerate(found):
        vinv[n : n + 1, :] = row
    to_smem = pltpu.make_async_copy(vinv, sinv, load_sem.at[2])
    to_smem.start()
    to_smem.wait()

    all_of(recv1, rsem.at[1])

    def order(j):
        ordf[j + 1] = recv1[sinv[0, j]]

    for_each(BLOCKS, order)
    edge_up = pltpu.make_async_remote_copy(
        src_ref=ordf.at[BLOCKS], dst_ref=ordf.at[0], send_sem=ssem.at[6], recv_sem=rsem.at[6],
        device_id=(ax, lax.rem(az + 1, AZ)), device_id_type=MESH,
    )
    edge_down = pltpu.make_async_remote_copy(
        src_ref=ordf.at[1], dst_ref=ordf.at[BLOCKS + 1], send_sem=ssem.at[7], recv_sem=rsem.at[7],
        device_id=(ax, lax.rem(az + AZ - 1, AZ)), device_id_type=MESH,
    )
    edge_up.start()
    edge_down.start()

    each_target(CUTS[0], CUTS[1], make_base, go_base)
    edge_up.wait_recv()
    edge_down.wait_recv()

    def gather(j):
        beside_faces[j] = (
            recv1[sinv[1, j + 64]] * weights[0]
            + recv1[sinv[2, j + 64]] * weights[1]
            + ordf[j] * weights[2]
            + ordf[j + 2] * weights[3]
        )

    for_each(BLOCKS, gather)

    def send_back(group):
        def one(i, carry):
            sax, saz = source_of(ax, az, i)
            s = sax * AZ + saz
            slot = jnp.where(s < 64, sinv[3, jnp.minimum(s, 63)], sinv[4, jnp.maximum(s - 64, 0)])
            send2[s] = beside_faces[jnp.minimum(slot, BLOCKS - 1)]
            pltpu.make_async_remote_copy(
                src_ref=send2.at[s], dst_ref=recv2.at[me], send_sem=ssem.at[5],
                recv_sem=back_sem.at[group], device_id=(sax, saz), device_id_type=MESH,
            ).start()
            return carry

        lax.fori_loop(EARLY + group * GROUP, EARLY + (group + 1) * GROUP, one, 0)

    for group in range(GROUPS):
        send_back(group)
    each_target(CUTS[1], EARLY, make_base, go_base)

    def finish(i, d):
        nearby = jnp.dot(unfold(recv2[d]), spread[...], preferred_element_type=F32)
        put(d, swept(sidx[0, d], nearby))

    def go_whole(i, d, where):
        push(send_a.at[d], recv_a.at[me], 2, where)
        push(send_b.at[d], recv_b.at[me], 3, where)

    def go_first(i, d, where):
        push(send_a.at[d], recv_a.at[me], 2, where)

    for group in range(GROUPS):
        all_of(recv2, back_sem.at[group], GROUP)
        each_target(EARLY + group * GROUP, EARLY + (group + 1) * GROUP, finish, go_whole if group < GROUPS - 1 else go_first)

    def send_rest(i, carry):
        tax, taz = target_of(ax, az, i)
        push(send_b.at[tax * AZ + taz], recv_b.at[me], 3, (tax, taz))
        return carry

    lax.fori_loop(DEVS - GROUP, DEVS, send_rest, 0)

    all_of(recv_t, rsem.at[4], EARLY - 1)

    def correct(j):
        s = sinv[0, j]
        none = jnp.zeros((16, 128), BF)
        t_low, t_high, t_side = recv_t[s, 0:16], recv_t[s, 16:32], recv_t[s, 32:48]
        rhs = jnp.concatenate(
            [
                jnp.concatenate([t_low, none, t_side, none], axis=0),
                jnp.concatenate([none, t_high, none, t_side], axis=0),
            ],
            axis=1,
        )
        update = jnp.dot(unfold(beside_faces[j]), rhs, preferred_element_type=F32) * diffusion
        stage[j] = update.reshape(3, 16, 256)

    for_each(BLOCKS, correct)

    all_of(recv_a, rsem.at[2])

    def add_a(j):
        final[j, 0:2] = (stage[j, 0:2] + recv_a[sinv[0, j]].astype(F32)).astype(BF)

    for_each(BLOCKS, add_a)
    all_of(recv_b, rsem.at[3])

    def add_b(n, carry):
        for k in range(UNROLL):
            j = n * UNROLL + k
            final[j, 2:3] = (stage[j, 2:3] + recv_b[sinv[0, j]].astype(F32)).astype(BF)
        return carry

    copies = []
    for g in range(4):
        lax.fori_loop(g * 16 // UNROLL, (g + 1) * 16 // UNROLL, add_b, 0)
        part = pl.ds(g * 16, 16)
        copies.append(pltpu.make_async_copy(final.at[part], out.at[part], out_sem.at[g]))
        copies[-1].start()

    all_of(meta_s, ssem.at[0])
    all_of(send1, ssem.at[1])
    all_of(recv_t, ssem.at[4], EARLY - 1)
    all_of(send2, ssem.at[5], DEVS - EARLY)
    all_of(send_a, ssem.at[2])
    all_of(send_b, ssem.at[3])
    edge_up.wait_send()
    edge_down.wait_send()
    for copy in copies:
        copy.wait()


def widen(narrow, wide, held, widened, in_sem, out_sem):
    size = BLOCKS // PARTS
    parts = [pl.ds(n * size, size) for n in range(PARTS)]
    loads = [pltpu.make_async_copy(narrow.at[p], held.at[p], in_sem.at[n]) for n, p in enumerate(parts)]
    stores = [pltpu.make_async_copy(widened.at[p], wide.at[p], out_sem.at[n]) for n, p in enumerate(parts)]
    for load in loads:
        load.start()
    for n in range(PARTS):
        loads[n].wait()

        def one(j, carry):
            for k in range(UNROLL):
                b = n * size + j * UNROLL + k
                widened[b] = held[b].astype(F32)
            return carry

        lax.fori_loop(0, size // UNROLL, one, 0)
        stores[n].start()
    for store in stores:
        store.wait()


def body(history, inverse_tiles, levels, destination):
    anywhere = pl.BlockSpec(memory_space=pl.ANY)
    moved = pl.pallas_call(
        kernel,
        out_shape=jax.ShapeDtypeStruct((BLOCKS, 3, 16, 256), BF),
        in_specs=[pl.BlockSpec(memory_space=pltpu.HBM)] * 4,
        out_specs=anywhere,
        scratch_shapes=[
            pltpu.VMEM((BLOCKS, 3, 16, 256), BF),
            pltpu.VMEM((BLOCKS, 6, 16, 256), BF),
            pltpu.VMEM((BLOCKS, 128, 128), BF),
            pltpu.VMEM((DEVS, 1, 128), jnp.int32),
            pltpu.VMEM((DEVS, 1, 128), jnp.int32),
            pltpu.VMEM((DEVS, FACES, 128), BF),
            pltpu.VMEM((DEVS, FACES, 128), BF),
            pltpu.VMEM((EARLY, 48, 128), BF),
            pltpu.VMEM((DEVS, 48, 128), BF),
            pltpu.VMEM((DEVS, FACES, 128), BF),
            pltpu.VMEM((DEVS, FACES, 128), BF),
            pltpu.VMEM((DEVS, 2, 16, 256), BF),
            pltpu.VMEM((DEVS, 2, 16, 256), BF),
            pltpu.VMEM((DEVS, 1, 16, 256), BF),
            pltpu.VMEM((DEVS, 1, 16, 256), BF),
            pltpu.VMEM((BLOCKS, 3, 16, 256), F32),
            pltpu.VMEM((BLOCKS, 3, 16, 256), BF),
            pltpu.VMEM((BLOCKS + 2, FACES, 128), BF),
            pltpu.VMEM((BLOCKS, FACES, 128), BF),
            pltpu.VMEM((256, 256), BF),
            pltpu.VMEM((3, 256, 128), BF),
            pltpu.VMEM((64, 256), BF),
            pltpu.VMEM((48, 128), BF),
            pltpu.VMEM((4, FACES, 128), BF),
            pltpu.SMEM((BLOCKS,), jnp.int32),
            pltpu.SMEM((BLOCKS,), jnp.int32),
            pltpu.VMEM((8, 128), jnp.int32),
            pltpu.SMEM((8, 128), jnp.int32),
            pltpu.VMEM((8, 128), jnp.int32),
            pltpu.SMEM((8, 128), jnp.int32),
            pltpu.SemaphoreType.DMA((6,)),
            pltpu.SemaphoreType.DMA((8,)),
            pltpu.SemaphoreType.DMA((8,)),
            pltpu.SemaphoreType.DMA((GROUPS,)),
            pltpu.SemaphoreType.DMA((4,)),
        ],
        compiler_params=pltpu.CompilerParams(
            collective_id=0, has_side_effects=True, vmem_limit_bytes=60 * 2**20
        ),
    )(history.reshape(BLOCKS, 9, 16, 256), inverse_tiles, destination, levels)
    return pl.pallas_call(
        widen,
        out_shape=jax.ShapeDtypeStruct((BLOCKS, 3, 16, 256), F32),
        in_specs=[pl.BlockSpec(memory_space=pltpu.HBM)],
        out_specs=pl.BlockSpec(memory_space=pltpu.HBM),
        scratch_shapes=[
            pltpu.VMEM((BLOCKS, 3, 16, 256), BF),
            pltpu.VMEM((BLOCKS, 3, 16, 256), F32),
            pltpu.SemaphoreType.DMA((PARTS,)),
            pltpu.SemaphoreType.DMA((PARTS,)),
        ],
        compiler_params=pltpu.CompilerParams(vmem_limit_bytes=60 * 2**20),
    )(moved)


def solution(mesh):
    placed = (
        P(("ax", "az"), None, None, None, None),
        P(("ax", "az"), None, None),
        P(("ax", "az")),
        P(("ax", "az")),
    )
    return jax.shard_map(
        body,
        mesh=mesh,
        in_specs=placed,
        out_specs=P(("ax", "az"), None, None, None),
        check_vma=False,
    )
```

```python
import functools

import jax
import jax.numpy as jnp
from jax import lax
from jax.experimental import pallas as pl
from jax.experimental.pallas import tpu as pltpu
from jax.sharding import PartitionSpec as P

diffusion = 0.04
MESH = pl.DeviceIdType.MESH
F32 = jnp.float32
BF = jnp.bfloat16

BLOCKS = 64
DEVS = 128
AZ = 8
FACES = 24
EARLY = 32
STRIDE = 81
UNROLL = 4
CUTS = (8, 20)
GROUPS = 3
GROUP = (DEVS - EARLY) // GROUPS
PARTS = 4
NONE = 127


def target_of(ax, az, i):
    o = lax.rem(i * STRIDE, DEVS)
    dc = lax.rem(o, 2)
    dy = lax.rem(lax.div(o, 2), 4)
    dx = lax.rem(lax.div(o, 8), 4)
    dz = lax.div(o, 32)
    z = lax.rem(lax.div(ax, 4) + dz, 4)
    x = lax.rem(lax.rem(ax, 4) + dx, 4)
    y = lax.rem(lax.div(az, 2) + dy, 4)
    c = lax.rem(lax.rem(az, 2) + dc, 2)
    return z * 4 + x, y * 2 + c


def source_of(ax, az, i):
    o = lax.rem(i * STRIDE, DEVS)
    dc = lax.rem(o, 2)
    dy = lax.rem(lax.div(o, 2), 4)
    dx = lax.rem(lax.div(o, 8), 4)
    dz = lax.div(o, 32)
    z = lax.rem(lax.div(ax, 4) - dz + 4, 4)
    x = lax.rem(lax.rem(ax, 4) - dx + 4, 4)
    y = lax.rem(lax.div(az, 2) - dy + 4, 4)
    c = lax.rem(lax.rem(az, 2) - dc + 2, 2)
    return z * 4 + x, y * 2 + c


def bf16_of(mask):
    return jnp.where(mask, 1.0, 0.0).astype(BF)


def fill_constants(nsel, fsel, spread, tsel, weights, ax):
    src = lax.broadcasted_iota(jnp.int32, (256, 256), 0)
    dst = lax.broadcasted_iota(jnp.int32, (256, 256), 1)
    ps, qs = lax.div(src, 16), lax.rem(src, 16)
    pd, qd = lax.div(dst, 16), lax.rem(dst, 16)
    beside = ((ps == pd) & (jnp.abs(qs - qd) == 1)) | ((qs == qd) & (jnp.abs(ps - pd) == 1))
    nsel[...] = bf16_of(beside)
    src = lax.broadcasted_iota(jnp.int32, (256, 128), 0)
    kk = lax.rem(lax.broadcasted_iota(jnp.int32, (256, 128), 1), 64)
    plane = jnp.where(kk < 48, 0, 8) + lax.rem(kk, 8)
    pick = jnp.where(
        kk < 16,
        240 + kk,
        jnp.where(kk < 32, kk - 16, plane * 16 + jnp.where(lax.rem(kk, 16) < 8, 15, 0)),
    )
    low, high = kk < 16, (kk >= 16) & (kk < 32)
    fsel[0] = bf16_of((src == pick) & low)
    fsel[1] = bf16_of((src == pick) & high)
    fsel[2] = bf16_of((src == pick) & (kk >= 32))
    row = lax.broadcasted_iota(jnp.int32, (48, 128), 0)
    col = lax.broadcasted_iota(jnp.int32, (48, 128), 1)
    pick = jnp.where(
        row < 16,
        row,
        jnp.where(row < 32, 96 + row, lax.rem(row, 8) * 16 + jnp.where(row < 40, 0, 15)),
    )
    tsel[...] = bf16_of(col == pick)
    kk = lax.broadcasted_iota(jnp.int32, (64, 256), 0)
    dst = lax.broadcasted_iota(jnp.int32, (64, 256), 1)
    plane = jnp.where(kk < 48, 0, 8) + lax.rem(kk, 8)
    pick = jnp.where(
        kk < 16,
        kk,
        jnp.where(kk < 32, 224 + kk, plane * 16 + jnp.where(lax.rem(kk, 16) < 8, 0, 15)),
    )
    spread[...] = bf16_of(dst == pick)
    kk = lax.rem(lax.broadcasted_iota(jnp.int32, (FACES, 128), 1), 64)
    weights[0] = bf16_of((kk < 16) & (ax > 0))
    weights[1] = bf16_of((kk >= 16) & (kk < 32) & (ax < 15))
    weights[2] = bf16_of((kk >= 32) & (lax.rem(kk, 16) < 8))
    weights[3] = bf16_of((kk >= 32) & (lax.rem(kk, 16) >= 8))


def kernel(
    hist, tiles, dest_any, lev_any, out,
    newest, older, tbuf, meta_s, meta_r, send1, recv1, send_t, recv_t, send2, recv2,
    send_a, recv_a, send_b, recv_b, stage, final, ordf, beside_faces,
    nsel, fsel, spread, tsel, weights, dest, lev, vidx, sidx, vinv, sinv,
    load_sem, ssem, rsem, back_sem, out_sem,
):
    ax = lax.axis_index("ax")
    az = lax.axis_index("az")
    me = ax * AZ + az
    barrier = pltpu.get_barrier_semaphore()

    load_d = pltpu.make_async_copy(dest_any, dest, load_sem.at[3])
    load_l = pltpu.make_async_copy(lev_any, lev, load_sem.at[4])
    load_h0 = pltpu.make_async_copy(hist.at[:, pl.ds(0, 3)], newest, load_sem.at[0])
    load_h = pltpu.make_async_copy(hist.at[:, pl.ds(3, 6)], older, load_sem.at[5])
    load_t = pltpu.make_async_copy(tiles, tbuf, load_sem.at[1])
    loads = (load_d, load_l, load_h0, load_t, load_h)
    for load in loads:
        load.start()

    def greet(i, carry):
        t = lax.rem(me + i, DEVS)
        there = (lax.div(t, AZ), lax.rem(t, AZ))
        pl.semaphore_signal(barrier, inc=1, device_id=there, device_id_type=MESH)
        return carry

    lax.fori_loop(1, DEVS, greet, 0)

    lane = lax.broadcasted_iota(jnp.int32, (1, 128), 1)

    def place(b, carry):
        which, slot = carry
        there = dest[b]
        hit = lane == lax.div(there, BLOCKS)
        return jnp.where(hit, b, which), jnp.where(hit, lax.rem(there, BLOCKS), slot)

    load_d.wait()
    load_l.wait()
    which, slot = lax.fori_loop(
        0, BLOCKS, place, (jnp.zeros((1, 128), jnp.int32), jnp.full((1, 128), NONE, jnp.int32))
    )
    vidx[0:1, :] = which
    vidx[1:2, :] = slot
    to_smem = pltpu.make_async_copy(vidx, sidx, load_sem.at[2])
    to_smem.start()
    fill_constants(nsel, fsel, spread, tsel, weights, ax)
    to_smem.wait()


    def scale_of(b):
        level = lev[b]
        return jnp.where(level == 0, 1.0, jnp.where(level == 1, 4.0, 16.0)).astype(F32)

    def swept(b, nearby=None):
        x = newest[b].reshape(48, 256)
        h0 = x.astype(F32)
        h1 = older[b, 0:3].reshape(48, 256).astype(F32)
        h2 = older[b, 3:6].reshape(48, 256).astype(F32)
        source = ((18.0 * h0 - 9.0 * h1 + 2.0 * h2) * (1.0 / 11.0)).astype(BF).astype(F32)
        c = diffusion * scale_of(b)
        radial = lax.rem(lax.broadcasted_iota(jnp.int32, (48, 256), 0), 16)
        beside = jnp.dot(x, nsel[...], preferred_element_type=F32)
        beside += jnp.where(radial == 0, 0.0, pltpu.roll(h0, 1, 0))
        beside += jnp.where(radial == 15, 0.0, pltpu.roll(h0, 47, 0))
        if nearby is not None:
            beside += nearby
        defect = (source - (1.0 + 6.0 * c) * h0 + c * beside).astype(BF)
        lhs = jnp.concatenate([defect[:, 0:128], defect[:, 128:256]], axis=0)
        u = lax.dot_general(lhs, tbuf[b], (((1,), (1,)), ((), ())), preferred_element_type=F32)
        return h0 + jnp.concatenate([u[0:48], u[48:96]], axis=1)

    def for_each(count, step):
        def some(n, carry):
            for k in range(UNROLL):
                step(n * UNROLL + k)
            return carry

        lax.fori_loop(0, count // UNROLL, some, 0)

    left16 = lax.broadcasted_iota(jnp.int32, (16, 128), 1) < 64
    left8 = lax.broadcasted_iota(jnp.int32, (8, 128), 1) < 64

    def pack_first(d):
        below = jnp.maximum(d - AZ, 0)
        above = jnp.minimum(d + AZ, DEVS - 1)
        slot_below = jnp.where(d >= AZ, sidx[1, below], NONE)
        slot_above = jnp.where(d < DEVS - AZ, sidx[1, above], NONE)
        meta_s[d] = jnp.where(lane < 64, sidx[1, d], slot_below * 128 + slot_above)
        own, low, high = sidx[0, d], sidx[0, below], sidx[0, above]
        faces = sum(
            jnp.dot(newest[b].reshape(48, 256), fsel[n], preferred_element_type=F32)
            for n, b in enumerate((low, high, own))
        )
        upper = jnp.where(left16, faces[0:16], faces[16:32])
        lower = jnp.where(left8, faces[32:40], faces[40:48])
        send1[d] = jnp.concatenate([upper, lower], axis=0).astype(BF)

    def columns_of(b):
        u = lax.dot_general(tsel[...], tbuf[b], (((1,), (1,)), ((), ())), preferred_element_type=F32)
        return (u * scale_of(b)).astype(BF)

    def unfold(packed):
        f = packed.astype(F32)
        parts = [f[0:16, 0:64], f[0:16, 64:128], f[16:24, 0:64], f[16:24, 64:128]]
        return jnp.concatenate(parts, axis=0).astype(BF)

    def push(src, dst, n, where):
        pltpu.make_async_remote_copy(
            src_ref=src, dst_ref=dst, send_sem=ssem.at[n], recv_sem=rsem.at[n],
            device_id=where, device_id_type=MESH,
        ).start()

    load_h0.wait()
    pl.semaphore_wait(barrier, DEVS - 1)

    def send_first(n, carry):
        targets = [target_of(ax, az, n * UNROLL + k) for k in range(UNROLL)]
        for tax, taz in targets:
            pack_first(tax * AZ + taz)
        for k, (tax, taz) in enumerate(targets):
            d = tax * AZ + taz

            def go():
                push(meta_s.at[d], meta_r.at[me], 0, (tax, taz))
                push(send1.at[d], recv1.at[me], 1, (tax, taz))

            if k > 0:
                go()
            else:
                pl.when(n > 0)(go)
        return carry

    lax.fori_loop(0, DEVS // UNROLL, send_first, 0)
    meta_r[me] = meta_s[me]
    recv1[me] = send1[me]

    load_t.wait()

    def each_target(low, high, make, go):
        def some(n, carry):
            items = [(n * UNROLL + k, target_of(ax, az, n * UNROLL + k)) for k in range(UNROLL)]
            for i, (tax, taz) in items:
                make(i, tax * AZ + taz)
            for i, (tax, taz) in items:
                go(i, tax * AZ + taz, (tax, taz))
            return carry

        lax.fori_loop(low // UNROLL, high // UNROLL, some, 0)

    def make_columns(i, d):
        send_t[i] = columns_of(sidx[0, d])

    def go_columns(i, d, where):
        pl.when(i > 0)(lambda: push(send_t.at[i], recv_t.at[me], 4, where))

    each_target(0, EARLY, make_columns, go_columns)
    recv_t[me] = send_t[0]

    def no_columns(i, carry):
        sax, saz = source_of(ax, az, i)
        recv_t[sax * AZ + saz] = jnp.zeros((48, 128), BF)
        return carry

    lax.fori_loop(EARLY, DEVS, no_columns, 0)

    load_h.wait()

    def put(d, field):
        field = field.astype(BF).reshape(3, 16, 256)
        send_a[d] = field[0:2]
        send_b[d] = field[2:3]

    def make_base(i, d):
        put(d, swept(sidx[0, d]))

    def go_base(i, d, where):
        def go():
            push(send_a.at[d], recv_a.at[me], 2, where)
            push(send_b.at[d], recv_b.at[me], 3, where)

        pl.when(i > 0)(go)

    each_target(0, CUTS[0], make_base, go_base)
    recv_a[me] = send_a[me]
    recv_b[me] = send_b[me]

    def all_of(ref, sem, count=DEVS - 1):
        part = ref.at[pl.ds(0, count)]
        pltpu.make_async_copy(part, part, sem).wait()

    all_of(meta_r, rsem.at[0])

    def unplace(s, carry):
        mine, low, high, slot_low, slot_high = carry
        code = meta_r[s]
        mine = jnp.where(code == lane, s, mine)
        low = jnp.where(lax.div(code, 128) == lane - 64, s, low)
        high = jnp.where(lax.rem(code, 128) == lane - 64, s, high)
        slot_low = jnp.where(lane == s, code, slot_low)
        slot_high = jnp.where(lane == s - 64, code, slot_high)
        return mine, low, high, slot_low, slot_high

    def unplace_some(n, carry):
        for k in range(UNROLL):
            carry = unplace(n * UNROLL + k, carry)
        return carry

    nothing = (jnp.zeros((1, 128), jnp.int32),) * 5
    found = lax.fori_loop(0, DEVS // UNROLL, unplace_some, nothing)
    for n, row in enumerate(found):
        vinv[n : n + 1, :] = row
    to_smem = pltpu.make_async_copy(vinv, sinv, load_sem.at[2])
    to_smem.start()
    to_smem.wait()

    all_of(recv1, rsem.at[1])

    def order(j):
        ordf[j + 1] = recv1[sinv[0, j]]

    for_each(BLOCKS, order)
    edge_up = pltpu.make_async_remote_copy(
        src_ref=ordf.at[BLOCKS], dst_ref=ordf.at[0], send_sem=ssem.at[6], recv_sem=rsem.at[6],
        device_id=(ax, lax.rem(az + 1, AZ)), device_id_type=MESH,
    )
    edge_down = pltpu.make_async_remote_copy(
        src_ref=ordf.at[1], dst_ref=ordf.at[BLOCKS + 1], send_sem=ssem.at[7], recv_sem=rsem.at[7],
        device_id=(ax, lax.rem(az + AZ - 1, AZ)), device_id_type=MESH,
    )
    edge_up.start()
    edge_down.start()

    each_target(CUTS[0], CUTS[1], make_base, go_base)
    edge_up.wait_recv()
    edge_down.wait_recv()

    def gather(j):
        beside_faces[j] = (
            recv1[sinv[1, j + 64]] * weights[0]
            + recv1[sinv[2, j + 64]] * weights[1]
            + ordf[j] * weights[2]
            + ordf[j + 2] * weights[3]
        )

    for_each(BLOCKS, gather)

    def send_back(group):
        def one(i, carry):
            sax, saz = source_of(ax, az, i)
            s = sax * AZ + saz
            slot = jnp.where(s < 64, sinv[3, jnp.minimum(s, 63)], sinv[4, jnp.maximum(s - 64, 0)])
            send2[s] = beside_faces[jnp.minimum(slot, BLOCKS - 1)]
            pltpu.make_async_remote_copy(
                src_ref=send2.at[s], dst_ref=recv2.at[me], send_sem=ssem.at[5],
                recv_sem=back_sem.at[group], device_id=(sax, saz), device_id_type=MESH,
            ).start()
            return carry

        lax.fori_loop(EARLY + group * GROUP, EARLY + (group + 1) * GROUP, one, 0)

    for group in range(GROUPS):
        send_back(group)
    each_target(CUTS[1], EARLY, make_base, go_base)

    def finish(i, d):
        nearby = jnp.dot(unfold(recv2[d]), spread[...], preferred_element_type=F32)
        put(d, swept(sidx[0, d], nearby))

    def go_whole(i, d, where):
        push(send_a.at[d], recv_a.at[me], 2, where)
        push(send_b.at[d], recv_b.at[me], 3, where)

    def go_first(i, d, where):
        push(send_a.at[d], recv_a.at[me], 2, where)

    for group in range(GROUPS):
        all_of(recv2, back_sem.at[group], GROUP)
        each_target(EARLY + group * GROUP, EARLY + (group + 1) * GROUP, finish, go_whole if group < GROUPS - 1 else go_first)

    def send_rest(i, carry):
        tax, taz = target_of(ax, az, i)
        push(send_b.at[tax * AZ + taz], recv_b.at[me], 3, (tax, taz))
        return carry

    lax.fori_loop(DEVS - GROUP, DEVS, send_rest, 0)

    all_of(recv_t, rsem.at[4], EARLY - 1)

    def correct(j):
        s = sinv[0, j]
        none = jnp.zeros((16, 128), BF)
        t_low, t_high, t_side = recv_t[s, 0:16], recv_t[s, 16:32], recv_t[s, 32:48]
        rhs = jnp.concatenate(
            [
                jnp.concatenate([t_low, none, t_side, none], axis=0),
                jnp.concatenate([none, t_high, none, t_side], axis=0),
            ],
            axis=1,
        )
        update = jnp.dot(unfold(beside_faces[j]), rhs, preferred_element_type=F32) * diffusion
        stage[j] = update.reshape(3, 16, 256)

    for_each(BLOCKS, correct)

    all_of(recv_a, rsem.at[2])

    def add_a(j):
        final[j, 0:2] = (stage[j, 0:2] + recv_a[sinv[0, j]].astype(F32)).astype(BF)

    for_each(BLOCKS, add_a)
    all_of(recv_b, rsem.at[3])

    def add_b(n, carry):
        for k in range(UNROLL):
            j = n * UNROLL + k
            final[j, 2:3] = (stage[j, 2:3] + recv_b[sinv[0, j]].astype(F32)).astype(BF)
        return carry

    copies = []
    for g in range(4):
        lax.fori_loop(g * 16 // UNROLL, (g + 1) * 16 // UNROLL, add_b, 0)
        part = pl.ds(g * 16, 16)
        copies.append(pltpu.make_async_copy(final.at[part], out.at[part], out_sem.at[g]))
        copies[-1].start()

    all_of(meta_s, ssem.at[0])
    all_of(send1, ssem.at[1])
    all_of(recv_t, ssem.at[4], EARLY - 1)
    all_of(send2, ssem.at[5], DEVS - EARLY)
    all_of(send_a, ssem.at[2])
    all_of(send_b, ssem.at[3])
    edge_up.wait_send()
    edge_down.wait_send()
    for copy in copies:
        copy.wait()


def widen(narrow, wide, held, widened, in_sem, out_sem):
    size = BLOCKS // PARTS
    parts = [pl.ds(n * size, size) for n in range(PARTS)]
    loads = [pltpu.make_async_copy(narrow.at[p], held.at[p], in_sem.at[n]) for n, p in enumerate(parts)]
    stores = [pltpu.make_async_copy(widened.at[p], wide.at[p], out_sem.at[n]) for n, p in enumerate(parts)]
    for load in loads:
        load.start()
    for n in range(PARTS):
        loads[n].wait()

        def one(j, carry):
            for k in range(UNROLL):
                b = n * size + j * UNROLL + k
                widened[b] = held[b].astype(F32)
            return carry

        lax.fori_loop(0, size // UNROLL, one, 0)
        stores[n].start()
    for store in stores:
        store.wait()


def body(history, inverse_tiles, levels, destination):
    anywhere = pl.BlockSpec(memory_space=pl.ANY)
    moved = pl.pallas_call(
        kernel,
        out_shape=jax.ShapeDtypeStruct((BLOCKS, 3, 16, 256), BF),
        in_specs=[pl.BlockSpec(memory_space=pltpu.HBM)] * 4,
        out_specs=anywhere,
        scratch_shapes=[
            pltpu.VMEM((BLOCKS, 3, 16, 256), BF),
            pltpu.VMEM((BLOCKS, 6, 16, 256), BF),
            pltpu.VMEM((BLOCKS, 128, 128), BF),
            pltpu.VMEM((DEVS, 1, 128), jnp.int32),
            pltpu.VMEM((DEVS, 1, 128), jnp.int32),
            pltpu.VMEM((DEVS, FACES, 128), BF),
            pltpu.VMEM((DEVS, FACES, 128), BF),
            pltpu.VMEM((EARLY, 48, 128), BF),
            pltpu.VMEM((DEVS, 48, 128), BF),
            pltpu.VMEM((DEVS, FACES, 128), BF),
            pltpu.VMEM((DEVS, FACES, 128), BF),
            pltpu.VMEM((DEVS, 2, 16, 256), BF),
            pltpu.VMEM((DEVS, 2, 16, 256), BF),
            pltpu.VMEM((DEVS, 1, 16, 256), BF),
            pltpu.VMEM((DEVS, 1, 16, 256), BF),
            pltpu.VMEM((BLOCKS, 3, 16, 256), F32),
            pltpu.VMEM((BLOCKS, 3, 16, 256), BF),
            pltpu.VMEM((BLOCKS + 2, FACES, 128), BF),
            pltpu.VMEM((BLOCKS, FACES, 128), BF),
            pltpu.VMEM((256, 256), BF),
            pltpu.VMEM((3, 256, 128), BF),
            pltpu.VMEM((64, 256), BF),
            pltpu.VMEM((48, 128), BF),
            pltpu.VMEM((4, FACES, 128), BF),
            pltpu.SMEM((BLOCKS,), jnp.int32),
            pltpu.SMEM((BLOCKS,), jnp.int32),
            pltpu.VMEM((8, 128), jnp.int32),
            pltpu.SMEM((8, 128), jnp.int32),
            pltpu.VMEM((8, 128), jnp.int32),
            pltpu.SMEM((8, 128), jnp.int32),
            pltpu.SemaphoreType.DMA((6,)),
            pltpu.SemaphoreType.DMA((8,)),
            pltpu.SemaphoreType.DMA((8,)),
            pltpu.SemaphoreType.DMA((GROUPS,)),
            pltpu.SemaphoreType.DMA((4,)),
        ],
        compiler_params=pltpu.CompilerParams(
            collective_id=0, has_side_effects=True, vmem_limit_bytes=60 * 2**20
        ),
    )(history.reshape(BLOCKS, 9, 16, 256), inverse_tiles, destination, levels)
    return pl.pallas_call(
        widen,
        out_shape=jax.ShapeDtypeStruct((BLOCKS, 3, 16, 256), F32),
        in_specs=[pl.BlockSpec(memory_space=pltpu.HBM)],
        out_specs=pl.BlockSpec(memory_space=pltpu.HBM),
        scratch_shapes=[
            pltpu.VMEM((BLOCKS, 3, 16, 256), BF),
            pltpu.VMEM((BLOCKS, 3, 16, 256), F32),
            pltpu.SemaphoreType.DMA((PARTS,)),
            pltpu.SemaphoreType.DMA((PARTS,)),
        ],
        compiler_params=pltpu.CompilerParams(vmem_limit_bytes=60 * 2**20),
    )(moved)


def solution(mesh):
    placed = (
        P(("ax", "az"), None, None, None, None),
        P(("ax", "az"), None, None),
        P(("ax", "az")),
        P(("ax", "az")),
    )
    return jax.shard_map(
        body,
        mesh=mesh,
        in_specs=placed,
        out_specs=P(("ax", "az"), None, None, None),
        check_vma=False,
    )
```

```python
import functools

import jax
import jax.numpy as jnp
from jax import lax
from jax.experimental import pallas as pl
from jax.experimental.pallas import tpu as pltpu
from jax.sharding import PartitionSpec as P

diffusion = 0.04
MESH = pl.DeviceIdType.MESH
F32 = jnp.float32
BF = jnp.bfloat16

BLOCKS = 64
DEVS = 128
AZ = 8
FACES = 24
EARLY = 44
STRIDE = 81
UNROLL = 4
CUTS = (8, 24)
GROUPS = 3
GROUP = (DEVS - EARLY) // GROUPS
PARTS = 4
NONE = 127


def target_of(ax, az, i):
    o = lax.rem(i * STRIDE, DEVS)
    dc = lax.rem(o, 2)
    dy = lax.rem(lax.div(o, 2), 4)
    dx = lax.rem(lax.div(o, 8), 4)
    dz = lax.div(o, 32)
    z = lax.rem(lax.div(ax, 4) + dz, 4)
    x = lax.rem(lax.rem(ax, 4) + dx, 4)
    y = lax.rem(lax.div(az, 2) + dy, 4)
    c = lax.rem(lax.rem(az, 2) + dc, 2)
    return z * 4 + x, y * 2 + c


def source_of(ax, az, i):
    o = lax.rem(i * STRIDE, DEVS)
    dc = lax.rem(o, 2)
    dy = lax.rem(lax.div(o, 2), 4)
    dx = lax.rem(lax.div(o, 8), 4)
    dz = lax.div(o, 32)
    z = lax.rem(lax.div(ax, 4) - dz + 4, 4)
    x = lax.rem(lax.rem(ax, 4) - dx + 4, 4)
    y = lax.rem(lax.div(az, 2) - dy + 4, 4)
    c = lax.rem(lax.rem(az, 2) - dc + 2, 2)
    return z * 4 + x, y * 2 + c


def bf16_of(mask):
    return jnp.where(mask, 1.0, 0.0).astype(BF)


def fill_constants(nsel, fsel, spread, tsel, weights, ax):
    src = lax.broadcasted_iota(jnp.int32, (256, 256), 0)
    dst = lax.broadcasted_iota(jnp.int32, (256, 256), 1)
    ps, qs = lax.div(src, 16), lax.rem(src, 16)
    pd, qd = lax.div(dst, 16), lax.rem(dst, 16)
    beside = ((ps == pd) & (jnp.abs(qs - qd) == 1)) | ((qs == qd) & (jnp.abs(ps - pd) == 1))
    nsel[...] = bf16_of(beside)
    src = lax.broadcasted_iota(jnp.int32, (256, 128), 0)
    kk = lax.rem(lax.broadcasted_iota(jnp.int32, (256, 128), 1), 64)
    plane = jnp.where(kk < 48, 0, 8) + lax.rem(kk, 8)
    pick = jnp.where(
        kk < 16,
        240 + kk,
        jnp.where(kk < 32, kk - 16, plane * 16 + jnp.where(lax.rem(kk, 16) < 8, 15, 0)),
    )
    low, high = kk < 16, (kk >= 16) & (kk < 32)
    fsel[0] = bf16_of((src == pick) & low)
    fsel[1] = bf16_of((src == pick) & high)
    fsel[2] = bf16_of((src == pick) & (kk >= 32))
    row = lax.broadcasted_iota(jnp.int32, (48, 128), 0)
    col = lax.broadcasted_iota(jnp.int32, (48, 128), 1)
    pick = jnp.where(
        row < 16,
        row,
        jnp.where(row < 32, 96 + row, lax.rem(row, 8) * 16 + jnp.where(row < 40, 0, 15)),
    )
    tsel[...] = bf16_of(col == pick)
    kk = lax.broadcasted_iota(jnp.int32, (64, 256), 0)
    dst = lax.broadcasted_iota(jnp.int32, (64, 256), 1)
    plane = jnp.where(kk < 48, 0, 8) + lax.rem(kk, 8)
    pick = jnp.where(
        kk < 16,
        kk,
        jnp.where(kk < 32, 224 + kk, plane * 16 + jnp.where(lax.rem(kk, 16) < 8, 0, 15)),
    )
    spread[...] = bf16_of(dst == pick)
    kk = lax.rem(lax.broadcasted_iota(jnp.int32, (FACES, 128), 1), 64)
    weights[0] = bf16_of((kk < 16) & (ax > 0))
    weights[1] = bf16_of((kk >= 16) & (kk < 32) & (ax < 15))
    weights[2] = bf16_of((kk >= 32) & (lax.rem(kk, 16) < 8))
    weights[3] = bf16_of((kk >= 32) & (lax.rem(kk, 16) >= 8))


def kernel(
    hist, tiles, dest_any, lev_any, out,
    newest, older, tbuf, meta_s, meta_r, send1, recv1, send_t, recv_t, send2, recv2,
    send_a, recv_a, send_b, recv_b, stage, final, ordf, beside_faces,
    nsel, fsel, spread, tsel, weights, dest, lev, vidx, sidx, vinv, sinv,
    load_sem, ssem, rsem, back_sem, out_sem,
):
    ax = lax.axis_index("ax")
    az = lax.axis_index("az")
    me = ax * AZ + az
    barrier = pltpu.get_barrier_semaphore()

    load_d = pltpu.make_async_copy(dest_any, dest, load_sem.at[3])
    load_l = pltpu.make_async_copy(lev_any, lev, load_sem.at[4])
    load_h0 = pltpu.make_async_copy(hist.at[:, pl.ds(0, 3)], newest, load_sem.at[0])
    load_h = pltpu.make_async_copy(hist.at[:, pl.ds(3, 6)], older, load_sem.at[5])
    load_t = pltpu.make_async_copy(tiles, tbuf, load_sem.at[1])
    loads = (load_d, load_l, load_h0, load_t, load_h)
    for load in loads:
        load.start()

    def greet(i, carry):
        t = jnp.where(i - 1 < me, i - 1, i)
        there = (lax.div(t, AZ), lax.rem(t, AZ))
        pl.semaphore_signal(barrier, inc=1, device_id=there, device_id_type=MESH)
        return carry

    lax.fori_loop(1, DEVS, greet, 0)

    lane = lax.broadcasted_iota(jnp.int32, (1, 128), 1)

    def place(b, carry):
        which, slot = carry
        there = dest[b]
        hit = lane == lax.div(there, BLOCKS)
        return jnp.where(hit, b, which), jnp.where(hit, lax.rem(there, BLOCKS), slot)

    load_d.wait()
    load_l.wait()
    which, slot = lax.fori_loop(
        0, BLOCKS, place, (jnp.zeros((1, 128), jnp.int32), jnp.full((1, 128), NONE, jnp.int32))
    )
    vidx[0:1, :] = which
    vidx[1:2, :] = slot
    to_smem = pltpu.make_async_copy(vidx, sidx, load_sem.at[2])
    to_smem.start()
    fill_constants(nsel, fsel, spread, tsel, weights, ax)
    to_smem.wait()


    def scale_of(b):
        level = lev[b]
        return jnp.where(level == 0, 1.0, jnp.where(level == 1, 4.0, 16.0)).astype(F32)

    def swept(b, nearby=None):
        x = newest[b].reshape(48, 256)
        h0 = x.astype(F32)
        h1 = older[b, 0:3].reshape(48, 256).astype(F32)
        h2 = older[b, 3:6].reshape(48, 256).astype(F32)
        source = ((18.0 * h0 - 9.0 * h1 + 2.0 * h2) * (1.0 / 11.0)).astype(BF).astype(F32)
        c = diffusion * scale_of(b)
        radial = lax.rem(lax.broadcasted_iota(jnp.int32, (48, 256), 0), 16)
        beside = jnp.dot(x, nsel[...], preferred_element_type=F32)
        beside += jnp.where(radial == 0, 0.0, pltpu.roll(h0, 1, 0))
        beside += jnp.where(radial == 15, 0.0, pltpu.roll(h0, 47, 0))
        if nearby is not None:
            beside += nearby
        defect = (source - (1.0 + 6.0 * c) * h0 + c * beside).astype(BF)
        lhs = jnp.concatenate([defect[:, 0:128], defect[:, 128:256]], axis=0)
        u = lax.dot_general(lhs, tbuf[b], (((1,), (1,)), ((), ())), preferred_element_type=F32)
        return h0 + jnp.concatenate([u[0:48], u[48:96]], axis=1)

    def for_each(count, step):
        def some(n, carry):
            for k in range(UNROLL):
                step(n * UNROLL + k)
            return carry

        lax.fori_loop(0, count // UNROLL, some, 0)

    left16 = lax.broadcasted_iota(jnp.int32, (16, 128), 1) < 64
    left8 = lax.broadcasted_iota(jnp.int32, (8, 128), 1) < 64

    def pack_first(d):
        below = jnp.maximum(d - AZ, 0)
        above = jnp.minimum(d + AZ, DEVS - 1)
        slot_below = jnp.where(d >= AZ, sidx[1, below], NONE)
        slot_above = jnp.where(d < DEVS - AZ, sidx[1, above], NONE)
        meta_s[d] = jnp.where(lane < 64, sidx[1, d], slot_below * 128 + slot_above)
        own, low, high = sidx[0, d], sidx[0, below], sidx[0, above]
        faces = sum(
            jnp.dot(newest[b].reshape(48, 256), fsel[n], preferred_element_type=F32)
            for n, b in enumerate((low, high, own))
        )
        upper = jnp.where(left16, faces[0:16], faces[16:32])
        lower = jnp.where(left8, faces[32:40], faces[40:48])
        send1[d] = jnp.concatenate([upper, lower], axis=0).astype(BF)

    def columns_of(b):
        u = lax.dot_general(tsel[...], tbuf[b], (((1,), (1,)), ((), ())), preferred_element_type=F32)
        return (u * scale_of(b)).astype(BF)

    def unfold(packed):
        f = packed.astype(F32)
        parts = [f[0:16, 0:64], f[0:16, 64:128], f[16:24, 0:64], f[16:24, 64:128]]
        return jnp.concatenate(parts, axis=0).astype(BF)

    def push(src, dst, n, where):
        pltpu.make_async_remote_copy(
            src_ref=src, dst_ref=dst, send_sem=ssem.at[n], recv_sem=rsem.at[n],
            device_id=where, device_id_type=MESH,
        ).start()

    load_h0.wait()
    pl.semaphore_wait(barrier, DEVS - 1)

    def send_first(n, carry):
        targets = [target_of(ax, az, n * UNROLL + k) for k in range(UNROLL)]
        for tax, taz in targets:
            pack_first(tax * AZ + taz)
        for k, (tax, taz) in enumerate(targets):
            d = tax * AZ + taz

            def go():
                push(meta_s.at[d], meta_r.at[me], 0, (tax, taz))
                push(send1.at[d], recv1.at[me], 1, (tax, taz))

            if k > 0:
                go()
            else:
                pl.when(n > 0)(go)
        return carry

    lax.fori_loop(0, DEVS // UNROLL, send_first, 0)
    meta_r[me] = meta_s[me]
    recv1[me] = send1[me]

    load_t.wait()

    def each_target(low, high, make, go):
        def some(n, carry):
            items = [(n * UNROLL + k, target_of(ax, az, n * UNROLL + k)) for k in range(UNROLL)]
            for i, (tax, taz) in items:
                make(i, tax * AZ + taz)
            for i, (tax, taz) in items:
                go(i, tax * AZ + taz, (tax, taz))
            return carry

        lax.fori_loop(low // UNROLL, high // UNROLL, some, 0)

    def make_columns(i, d):
        send_t[i] = columns_of(sidx[0, d])

    def go_columns(i, d, where):
        pl.when(i > 0)(lambda: push(send_t.at[i], recv_t.at[me], 4, where))

    each_target(0, EARLY, make_columns, go_columns)
    recv_t[me] = send_t[0]

    def no_columns(i, carry):
        sax, saz = source_of(ax, az, i)
        recv_t[sax * AZ + saz] = jnp.zeros((48, 128), BF)
        return carry

    lax.fori_loop(EARLY, DEVS, no_columns, 0)

    load_h.wait()

    def put(d, field):
        field = field.astype(BF).reshape(3, 16, 256)
        send_a[d] = field[0:2]
        send_b[d] = field[2:3]

    def make_base(i, d):
        put(d, swept(sidx[0, d]))

    def go_base(i, d, where):
        def go():
            push(send_a.at[d], recv_a.at[me], 2, where)
            push(send_b.at[d], recv_b.at[me], 3, where)

        pl.when(i > 0)(go)

    each_target(0, CUTS[0], make_base, go_base)
    recv_a[me] = send_a[me]
    recv_b[me] = send_b[me]

    def all_of(ref, sem, count=DEVS - 1):
        part = ref.at[pl.ds(0, count)]
        pltpu.make_async_copy(part, part, sem).wait()

    all_of(meta_r, rsem.at[0])

    def unplace(s, carry):
        mine, low, high, slot_low, slot_high = carry
        code = meta_r[s]
        mine = jnp.where(code == lane, s, mine)
        low = jnp.where(lax.div(code, 128) == lane - 64, s, low)
        high = jnp.where(lax.rem(code, 128) == lane - 64, s, high)
        slot_low = jnp.where(lane == s, code, slot_low)
        slot_high = jnp.where(lane == s - 64, code, slot_high)
        return mine, low, high, slot_low, slot_high

    def unplace_some(n, carry):
        for k in range(UNROLL):
            carry = unplace(n * UNROLL + k, carry)
        return carry

    nothing = (jnp.zeros((1, 128), jnp.int32),) * 5
    found = lax.fori_loop(0, DEVS // UNROLL, unplace_some, nothing)
    for n, row in enumerate(found):
        vinv[n : n + 1, :] = row
    to_smem = pltpu.make_async_copy(vinv, sinv, load_sem.at[2])
    to_smem.start()
    to_smem.wait()

    all_of(recv1, rsem.at[1])

    def order(j):
        ordf[j + 1] = recv1[sinv[0, j]]

    for_each(BLOCKS, order)
    edge_up = pltpu.make_async_remote_copy(
        src_ref=ordf.at[BLOCKS], dst_ref=ordf.at[0], send_sem=ssem.at[6], recv_sem=rsem.at[6],
        device_id=(ax, lax.rem(az + 1, AZ)), device_id_type=MESH,
    )
    edge_down = pltpu.make_async_remote_copy(
        src_ref=ordf.at[1], dst_ref=ordf.at[BLOCKS + 1], send_sem=ssem.at[7], recv_sem=rsem.at[7],
        device_id=(ax, lax.rem(az + AZ - 1, AZ)), device_id_type=MESH,
    )
    edge_up.start()
    edge_down.start()

    each_target(CUTS[0], CUTS[1], make_base, go_base)
    edge_up.wait_recv()
    edge_down.wait_recv()

    def gather(j):
        beside_faces[j] = (
            recv1[sinv[1, j + 64]] * weights[0]
            + recv1[sinv[2, j + 64]] * weights[1]
            + ordf[j] * weights[2]
            + ordf[j + 2] * weights[3]
        )

    for_each(BLOCKS, gather)

    def send_back(group):
        def one(i, carry):
            sax, saz = source_of(ax, az, i)
            s = sax * AZ + saz
            slot = jnp.where(s < 64, sinv[3, jnp.minimum(s, 63)], sinv[4, jnp.maximum(s - 64, 0)])
            send2[s] = beside_faces[jnp.minimum(slot, BLOCKS - 1)]
            pltpu.make_async_remote_copy(
                src_ref=send2.at[s], dst_ref=recv2.at[me], send_sem=ssem.at[5],
                recv_sem=back_sem.at[group], device_id=(sax, saz), device_id_type=MESH,
            ).start()
            return carry

        lax.fori_loop(EARLY + group * GROUP, EARLY + (group + 1) * GROUP, one, 0)

    for group in range(GROUPS):
        send_back(group)
    each_target(CUTS[1], EARLY, make_base, go_base)

    def finish(i, d):
        nearby = jnp.dot(unfold(recv2[d]), spread[...], preferred_element_type=F32)
        put(d, swept(sidx[0, d], nearby))

    def go_whole(i, d, where):
        push(send_a.at[d], recv_a.at[me], 2, where)
        push(send_b.at[d], recv_b.at[me], 3, where)

    def go_first(i, d, where):
        push(send_a.at[d], recv_a.at[me], 2, where)

    for group in range(GROUPS):
        all_of(recv2, back_sem.at[group], GROUP)
        each_target(EARLY + group * GROUP, EARLY + (group + 1) * GROUP, finish, go_whole if group < GROUPS - 1 else go_first)

    def send_rest(i, carry):
        tax, taz = target_of(ax, az, i)
        push(send_b.at[tax * AZ + taz], recv_b.at[me], 3, (tax, taz))
        return carry

    lax.fori_loop(DEVS - GROUP, DEVS, send_rest, 0)

    all_of(recv_t, rsem.at[4], EARLY - 1)

    def correct(j):
        s = sinv[0, j]
        none = jnp.zeros((16, 128), BF)
        t_low, t_high, t_side = recv_t[s, 0:16], recv_t[s, 16:32], recv_t[s, 32:48]
        rhs = jnp.concatenate(
            [
                jnp.concatenate([t_low, none, t_side, none], axis=0),
                jnp.concatenate([none, t_high, none, t_side], axis=0),
            ],
            axis=1,
        )
        update = jnp.dot(unfold(beside_faces[j]), rhs, preferred_element_type=F32) * diffusion
        stage[j] = update.reshape(3, 16, 256)

    for_each(BLOCKS, correct)

    all_of(recv_a, rsem.at[2])

    def add_a(j):
        final[j, 0:2] = (stage[j, 0:2] + recv_a[sinv[0, j]].astype(F32)).astype(BF)

    for_each(BLOCKS, add_a)
    all_of(recv_b, rsem.at[3])

    def add_b(n, carry):
        for k in range(UNROLL):
            j = n * UNROLL + k
            final[j, 2:3] = (stage[j, 2:3] + recv_b[sinv[0, j]].astype(F32)).astype(BF)
        return carry

    copies = []
    for g in range(4):
        lax.fori_loop(g * 16 // UNROLL, (g + 1) * 16 // UNROLL, add_b, 0)
        part = pl.ds(g * 16, 16)
        copies.append(pltpu.make_async_copy(final.at[part], out.at[part], out_sem.at[g]))
        copies[-1].start()

    all_of(meta_s, ssem.at[0])
    all_of(send1, ssem.at[1])
    all_of(recv_t, ssem.at[4], EARLY - 1)
    all_of(send2, ssem.at[5], DEVS - EARLY)
    all_of(send_a, ssem.at[2])
    all_of(send_b, ssem.at[3])
    edge_up.wait_send()
    edge_down.wait_send()
    for copy in copies:
        copy.wait()


def widen(narrow, wide, held, widened, in_sem, out_sem):
    size = BLOCKS // PARTS
    parts = [pl.ds(n * size, size) for n in range(PARTS)]
    loads = [pltpu.make_async_copy(narrow.at[p], held.at[p], in_sem.at[n]) for n, p in enumerate(parts)]
    stores = [pltpu.make_async_copy(widened.at[p], wide.at[p], out_sem.at[n]) for n, p in enumerate(parts)]
    for load in loads:
        load.start()
    for n in range(PARTS):
        loads[n].wait()

        def one(j, carry):
            for k in range(UNROLL):
                b = n * size + j * UNROLL + k
                widened[b] = held[b].astype(F32)
            return carry

        lax.fori_loop(0, size // UNROLL, one, 0)
        stores[n].start()
    for store in stores:
        store.wait()


def body(history, inverse_tiles, levels, destination):
    anywhere = pl.BlockSpec(memory_space=pl.ANY)
    moved = pl.pallas_call(
        kernel,
        out_shape=jax.ShapeDtypeStruct((BLOCKS, 3, 16, 256), BF),
        in_specs=[pl.BlockSpec(memory_space=pltpu.HBM)] * 4,
        out_specs=anywhere,
        scratch_shapes=[
            pltpu.VMEM((BLOCKS, 3, 16, 256), BF),
            pltpu.VMEM((BLOCKS, 6, 16, 256), BF),
            pltpu.VMEM((BLOCKS, 128, 128), BF),
            pltpu.VMEM((DEVS, 1, 128), jnp.int32),
            pltpu.VMEM((DEVS, 1, 128), jnp.int32),
            pltpu.VMEM((DEVS, FACES, 128), BF),
            pltpu.VMEM((DEVS, FACES, 128), BF),
            pltpu.VMEM((EARLY, 48, 128), BF),
            pltpu.VMEM((DEVS, 48, 128), BF),
            pltpu.VMEM((DEVS, FACES, 128), BF),
            pltpu.VMEM((DEVS, FACES, 128), BF),
            pltpu.VMEM((DEVS, 2, 16, 256), BF),
            pltpu.VMEM((DEVS, 2, 16, 256), BF),
            pltpu.VMEM((DEVS, 1, 16, 256), BF),
            pltpu.VMEM((DEVS, 1, 16, 256), BF),
            pltpu.VMEM((BLOCKS, 3, 16, 256), F32),
            pltpu.VMEM((BLOCKS, 3, 16, 256), BF),
            pltpu.VMEM((BLOCKS + 2, FACES, 128), BF),
            pltpu.VMEM((BLOCKS, FACES, 128), BF),
            pltpu.VMEM((256, 256), BF),
            pltpu.VMEM((3, 256, 128), BF),
            pltpu.VMEM((64, 256), BF),
            pltpu.VMEM((48, 128), BF),
            pltpu.VMEM((4, FACES, 128), BF),
            pltpu.SMEM((BLOCKS,), jnp.int32),
            pltpu.SMEM((BLOCKS,), jnp.int32),
            pltpu.VMEM((8, 128), jnp.int32),
            pltpu.SMEM((8, 128), jnp.int32),
            pltpu.VMEM((8, 128), jnp.int32),
            pltpu.SMEM((8, 128), jnp.int32),
            pltpu.SemaphoreType.DMA((6,)),
            pltpu.SemaphoreType.DMA((8,)),
            pltpu.SemaphoreType.DMA((8,)),
            pltpu.SemaphoreType.DMA((GROUPS,)),
            pltpu.SemaphoreType.DMA((4,)),
        ],
        compiler_params=pltpu.CompilerParams(
            collective_id=0, has_side_effects=True, vmem_limit_bytes=60 * 2**20
        ),
    )(history.reshape(BLOCKS, 9, 16, 256), inverse_tiles, destination, levels)
    return pl.pallas_call(
        widen,
        out_shape=jax.ShapeDtypeStruct((BLOCKS, 3, 16, 256), F32),
        in_specs=[pl.BlockSpec(memory_space=pltpu.HBM)],
        out_specs=pl.BlockSpec(memory_space=pltpu.HBM),
        scratch_shapes=[
            pltpu.VMEM((BLOCKS, 3, 16, 256), BF),
            pltpu.VMEM((BLOCKS, 3, 16, 256), F32),
            pltpu.SemaphoreType.DMA((PARTS,)),
            pltpu.SemaphoreType.DMA((PARTS,)),
        ],
        compiler_params=pltpu.CompilerParams(vmem_limit_bytes=60 * 2**20),
    )(moved)


def solution(mesh):
    placed = (
        P(("ax", "az"), None, None, None, None),
        P(("ax", "az"), None, None),
        P(("ax", "az")),
        P(("ax", "az")),
    )
    return jax.shard_map(
        body,
        mesh=mesh,
        in_specs=placed,
        out_specs=P(("ax", "az"), None, None, None),
        check_vma=False,
    )
```
